512 devices in a mesh: feat: 64 (over z_lo, y, core), tok: 8 (over z_hi, x).
Axes of the slice: x: 4, y: 4, z: 16 (z_hi: 2, z_lo: 8; z = z_hi * 8 + z_lo), core: 2. Of those that a mesh axis runs over, the one named last changes fastest.
Arguments:
- source: bfloat16 [1024, 3584], P(('tok', 'feat')), may hold values from -6 to 6
- target: bfloat16 [1024, 3584], P(('tok', 'feat')), may hold values from -6 to 6
- enc_weight: bfloat16 [3584, 16384], P('tok', 'feat'), may hold values from -0.09375 to 0.09375
- enc_bias: float32 [16384], P('feat'), may hold values from -3 to 3
- dec_weight: bfloat16 [16384, 3584], P('feat', 'tok'), may hold values from -0.09375 to 0.09375
- active: int32 [1024, 16384], P('tok', 'feat'), may hold values 0 or 1
Outputs:
- recon_error: float32 [1024, 3584], P(('tok', 'feat'))
- grad_enc: bfloat16 [3584, 16384], P(None, 'feat')
- grad_bias: float32 [16384], P('feat')
- grad_dec: bfloat16 [16384, 3584], P('feat')
The draws below stay inside these ranges and needn't reach their ends.
All inputs are finite; a program needn't handle non-finite values. No bound on the sum of `active` on one device may be relied on, other than what follows from the above.
Results may differ from the reference program's by a relative error of at most 0.019.
Values may be sent and summed in bfloat16 or wider, within the bound.
A program may use at most 64 MiB of HBM per device.

```python
import math
import jax
import jax.numpy as jnp
from jax import lax

D = 3584
F = 16384
TOK_DEV = 128
TOKENS = 1024
N_TOK = 8


def plant(values, rng, low, top_value):
    longest = values.shape.index(max(values.shape))
    spots = []
    for shift in (0, 1):
        where = [jax.random.randint(jax.random.fold_in(rng, axis), (), 0, length) for axis, length in enumerate(values.shape)]
        where[longest] = (where[longest] + shift) % values.shape[longest]
        spots.append(tuple(where))
    return values.at[spots[0]].set(low).at[spots[1]].set(top_value)


def shard_levels(rng, shape, cuts, smallest, largest):
    loudness = 1.0
    for position, parts in cuts:
        draws = jax.random.uniform(jax.random.fold_in(jax.random.fold_in(rng, 6), position), (parts,), jnp.float32, smallest / len(cuts), largest / len(cuts))
        loudness = loudness * jnp.repeat(jnp.exp(draws), shape[position] // parts).reshape((-1,) + (1,) * (len(shape) - 1 - position))
    return loudness


def gaussian(stream_key, extent, width, limit, shards=(), dtype=jnp.bfloat16):
    result = width * jax.random.normal(stream_key, extent, jnp.float32)
    if shards:
        result = result * shard_levels(stream_key, extent, shards, -0.22, 0.18)
    return jnp.clip(result, -limit, limit).astype(dtype)


def setup_inputs(seed: int = 0) -> dict:
    key_of = jax.random.split(jax.random.key(seed), 7)
    source = gaussian(key_of[0], (TOKENS, D), 1.0, 6.0, ((0, 512),))
    target = gaussian(key_of[1], (TOKENS, D), 1.0, 6.0, ((0, 512),))
    enc_weight = gaussian(key_of[2], (D, F), D ** -0.5, 0.09375, ((0, 8), (1, 64)))
    enc_bias = gaussian(key_of[3], (F,), 0.5, 3.0, ((0, 64),), jnp.float32)
    dec_weight = gaussian(key_of[4], (F, D), (F // 4) ** -0.5, 0.09375, ((0, 64), (1, 8)))
    active = plant((jax.random.randint(key_of[5], (TOKENS, F), 0, 4) < 1).astype(jnp.int32), jax.random.fold_in(key_of[5], 1), 0, 1)
    return dict(source=source, target=target, enc_weight=enc_weight, enc_bias=enc_bias, dec_weight=dec_weight, active=active)


def rounded(value):
    return lax.optimization_barrier(value.astype(jnp.bfloat16)).astype(jnp.float32)

def reference(source, target, enc_weight, enc_bias, dec_weight, active):
    gating = active.astype(jnp.float32)
    preact = jnp.dot(source, enc_weight, preferred_element_type=jnp.float32) + enc_bias
    features = (gating * preact).astype(jnp.bfloat16)
    recon = jnp.dot(features, dec_weight, preferred_element_type=jnp.float32)
    recon_error = recon - target.astype(jnp.float32)
    signal = (recon_error * (1.0 / math.sqrt(TOKENS))).astype(jnp.bfloat16)
    backflow = jnp.dot(signal, dec_weight.T, preferred_element_type=jnp.float32)
    pre_grad = gating * backflow
    pre_round = pre_grad.astype(jnp.bfloat16)
    enc_total = jnp.zeros((D, F), jnp.float32)
    dec_total = jnp.zeros((F, D), jnp.float32)
    bias_total = jnp.zeros((F,), jnp.float32)
    for group in range(N_TOK):
        lower = group * TOK_DEV
        upper = lower + TOK_DEV
        enc_total = enc_total + rounded(jnp.dot(source[lower:upper].T, pre_round[lower:upper], preferred_element_type=jnp.float32))
        dec_total = dec_total + rounded(jnp.dot(features[lower:upper].T, signal[lower:upper], preferred_element_type=jnp.float32))
        bias_total = bias_total + rounded(lax.optimization_barrier(jnp.sum(pre_grad[lower:upper], axis=0)))
    return (recon_error, enc_total.astype(jnp.bfloat16), bias_total, dec_total.astype(jnp.bfloat16))
```

```python
import math

import jax
import jax.numpy as jnp
from jax import lax
from jax.experimental import pallas as pl
from jax.experimental.pallas import tpu as pltpu
from jax.sharding import PartitionSpec as P

BF = jnp.bfloat16
F32 = jnp.float32
W = 448


def kernel(st_ref, enc_ref, bias_ref, dec_ref, act_ref, err_ref, ge_ref, gb_ref, gd_ref,
           st_in, st_rows, S, G, wt, dt, gate, pre, feats, prnd, part, r0, r1, r2, ebuf, ss, rs):
    tok = lax.axis_index("tok")
    feat = lax.axis_index("feat")
    zh, x = tok // 4, tok % 4
    zlo, y, c = feat // 8, (feat // 2) % 4, feat % 2
    z = zh * 8 + zlo
    zq, zr = z // 4, z % 4

    def dev(x_=None, y_=None, z_=None, c_=None):
        x_ = x if x_ is None else x_
        y_ = y if y_ is None else y_
        z_ = z if z_ is None else z_
        c_ = c if c_ is None else c_
        return {"tok": (z_ // 8) * 4 + x_, "feat": ((z_ % 8) * 4 + y_) * 2 + c_}

    def tok_dev(d):
        return {"tok": (tok + d) % 8, "feat": feat}

    zoff = (1, 15, 2)
    zback = (15, 1, 14)

    barrier = pltpu.get_barrier_semaphore()
    greet = [tok_dev(d) for d in range(1, 8)]
    greet += [dev(z_=(z + 4 * d) % 16) for d in (1, 3)]
    greet += [dev(z_=(z + d) % 16) for d in zback]
    greet += [dev(y_=(y + d) % 4) for d in (1, 2, 3)]
    greet += [dev(c_=1 - c)]
    greet += [dev(z_=zh * 8 + (zlo + d) % 8) for d in range(1, 8)]
    for g in greet:
        pl.semaphore_signal(barrier, inc=1, device_id=g, device_id_type=pl.DeviceIdType.MESH)

    nxt = [0]
    sent = []

    def send(src, dst, to):
        i = nxt[0]
        nxt[0] += 1
        cp = pltpu.make_async_remote_copy(
            src_ref=src, dst_ref=dst, send_sem=ss.at[i], recv_sem=rs.at[i],
            device_id=to, device_id_type=pl.DeviceIdType.MESH)
        cp.start()
        sent.append(cp)
        return cp

    def arrive(cps):
        for cp in cps:
            cp.wait_recv()

    me = x * 2 + zh
    wt[me, 0:W, :] = enc_ref[...]
    wt[me, W:W + 128, :] = act_ref[...].astype(F32).astype(BF)
    dt[me] = dec_ref[...]
    pl.semaphore_wait(barrier, len(greet))

    ex = [send(st_ref.at[(tok + d) % 8], st_in.at[tok], tok_dev(d)) for d in range(1, 8)]
    wz = send(wt.at[me], wt.at[me], dev(z_=(z + 8) % 16))
    st_in[tok] = st_ref[tok]
    arrive(ex)
    for k in range(8):
        v = st_in[k]
        st_rows[0, 2 * k:2 * k + 2, :] = v[0:2]
        st_rows[1, 2 * k:2 * k + 2, :] = v[2:4]

    cyx = (c * 4 + y) * 4 + x
    base = cyx * 4

    def gather_z(buf):
        own = buf.at[base + zq, zr]
        arrive([send(own, own, dev(z_=(z + 4 * d) % 16)) for d in (1, 3, 2)])
        col = buf.at[pl.ds(base, 4), zr]
        arrive([send(col, col, dev(z_=(z + d) % 16)) for d in zoff])

    def gather_x(buf):
        blk = buf.at[pl.ds(base, 4)]
        return [send(blk, blk, dev(x_=(x + d) % 4)) for d in (1, 3, 2)]

    def gather_y(buf):
        blk = buf.at[pl.ds((c * 4 + y) * 16, 16)]
        return [send(blk, blk, dev(y_=(y + d) % 4)) for d in (1, 3, 2)]

    def gather_c(buf):
        blk = buf.at[pl.ds(c * 64, 64)]
        return [send(blk, blk, dev(c_=1 - c))]

    S[base + zq, zr] = st_rows[0].astype(BF)
    gather_z(S)
    sx = gather_x(S)
    arrive([wz])
    pair = wt.at[pl.ds(2 * x, 2)]
    wx = [send(pair, pair, dev(x_=(x + d) % 4)) for d in (1, 3, 2)]
    arrive(sx)
    sy = gather_y(S)
    dz = send(dt.at[me], dt.at[me], dev(z_=(z + 8) % 16))
    arrive(wx)

    for h in range(2):
        n = lax.broadcasted_iota(jnp.int32, (512, 128), 0)
        m = lax.broadcasted_iota(jnp.int32, (512, 128), 1)
        fidx = (((n // 16) % 8) * 4 + n // 128) * 2 + h
        want = fidx * 2 + n % 2
        tn = (n // 2) % 8
        acc = jnp.zeros((512, 256), F32)
        for t in range(8):
            perm = jnp.where((m == want) & (tn == t), 1.0, 0.0).astype(BF)
            acc += jnp.dot(perm, wt[(t % 4) * 2 + t // 4, W:W + 128, :], preferred_element_type=F32)
        gate[h] = acc

    def rows(buf, h, k):
        return jnp.concatenate(
            [buf[pl.ds(((h * 4 + yy) * 4 + k // 2) * 4 + (k % 2) * 2, 2)].reshape(128, W) for yy in range(4)],
            axis=0)

    def encode(h):
        pre[...] = jnp.zeros((512, 256), F32)

        def step(k, _):
            pre[...] += jnp.dot(rows(S, h, k), wt[k, 0:W, :], preferred_element_type=F32)
            return 0

        lax.fori_loop(0, 8, step, 0)
        feats[h] = (gate[h] * (pre[...] + bias_ref[...])).astype(BF)

    def decode(h):
        r = lax.dot_general(feats[h], dt[me], (((1,), (1,)), ((), ())), preferred_element_type=F32)
        part[h] = r.reshape(4, 8, 16, W)

    arrive(sy)
    sc = gather_c(S)
    encode(c)
    arrive(sc)
    encode(1 - c)
    decode(1 - c)
    pc = send(part.at[1 - c], r0, dev(c_=1 - c))
    arrive([dz])
    dpair = dt.at[pl.ds(2 * x, 2)]
    dx = [send(dpair, dpair, dev(x_=(x + d) % 4)) for d in (1, 3, 2)]
    decode(c)
    arrive([pc])
    py = []
    for d in (2, 1, 3):
        yy = (y + d) % 4
        part[c, yy] = part[c, yy] + r0[yy]
        py.append(send(part.at[c, yy], r1.at[d], dev(y_=yy)))
    arrive(py)
    part[c, y] = part[c, y] + r0[y] + r1[1] + r1[2] + r1[3]
    pz = [send(part.at[c, y, (zlo + d) % 8], r2.at[d], dev(z_=zh * 8 + (zlo + d) % 8)) for d in range(1, 8)]
    arrive(pz)
    recon = part[c, y, zlo]
    for d in range(1, 8):
        recon = recon + r2[d]
    err = recon - st_rows[1]
    G[base + zq, zr] = (err * (1.0 / 32.0)).astype(BF)
    for k in range(8):
        ebuf[k] = err[2 * k:2 * k + 2]
    err_ref[tok] = ebuf[tok]
    eo = [send(ebuf.at[(tok + d) % 8], err_ref.at[tok], tok_dev(d)) for d in range(1, 8)]
    gather_z(G)
    arrive(gather_x(G))
    gy = gather_y(G)
    arrive(dx)
    arrive(gy)
    gc = gather_c(G)

    def back(h):
        pre[...] = jnp.zeros((512, 256), F32)

        def step(k, _):
            pre[...] += jnp.dot(rows(G, h, k), dt[k], preferred_element_type=F32)
            return 0

        lax.fori_loop(0, 8, step, 0)
        g = gate[h] * pre[...]
        prnd[h] = g.astype(BF)
        return jnp.sum(g, axis=0, keepdims=True)

    b0 = back(c)
    arrive(gc)
    gb_ref[...] = b0 + back(1 - c)

    def grads(k, _):
        t = (k % 2) * 4 + k // 2
        ge = jnp.zeros((W, 256), F32)
        gd = jnp.zeros((256, W), F32)
        for h in range(2):
            ge += lax.dot_general(rows(S, h, k), prnd[h], (((0,), (0,)), ((), ())), preferred_element_type=F32)
            gd += lax.dot_general(feats[h], rows(G, h, k), (((0,), (0,)), ((), ())), preferred_element_type=F32)
        ge_ref[t] = ge.astype(BF)
        gd_ref[t] = gd.astype(BF)
        return 0

    lax.fori_loop(0, 8, grads, 0)
    arrive(eo)
    for cp in sent:
        cp.wait_send()


def on_device(source, target, enc_weight, enc_bias, dec_weight, active):
    st = jnp.concatenate([source, target], axis=0).astype(F32)
    st = st.reshape(4, 8, W).transpose(1, 0, 2)
    vm = pl.BlockSpec(memory_space=pltpu.VMEM)
    err, ge, gb, gd = pl.pallas_call(
        kernel,
        out_shape=(
            jax.ShapeDtypeStruct((8, 2, W), F32),
            jax.ShapeDtypeStruct((8, W, 256), BF),
            jax.ShapeDtypeStruct((1, 256), F32),
            jax.ShapeDtypeStruct((8, 256, W), BF),
        ),
        in_specs=[vm] * 5,
        out_specs=[vm] * 4,
        scratch_shapes=[
            pltpu.VMEM((8, 4, W), F32),
            pltpu.VMEM((2, 16, W), F32),
            pltpu.VMEM((128, 4, 16, W), BF),
            pltpu.VMEM((128, 4, 16, W), BF),
            pltpu.VMEM((8, W + 128, 256), BF),
            pltpu.VMEM((8, W, 256), BF),
            pltpu.VMEM((2, 512, 256), F32),
            pltpu.VMEM((512, 256), F32),
            pltpu.VMEM((2, 512, 256), BF),
            pltpu.VMEM((2, 512, 256), BF),
            pltpu.VMEM((2, 4, 8, 16, W), F32),
            pltpu.VMEM((4, 8, 16, W), F32),
            pltpu.VMEM((4, 8, 16, W), F32),
            pltpu.VMEM((8, 16, W), F32),
            pltpu.VMEM((8, 2, W), F32),
            pltpu.SemaphoreType.DMA((72,)),
            pltpu.SemaphoreType.DMA((72,)),
        ],
        compiler_params=pltpu.CompilerParams(
            collective_id=0, has_side_effects=True, vmem_limit_bytes=56 * 1024 * 1024),
    )(st, enc_weight, enc_bias.reshape(1, 256), dec_weight.T, active)
    err = err.transpose(1, 0, 2).reshape(2, 8 * W)
    return (err, ge.reshape(8 * W, 256), gb.reshape(256), gd.transpose(1, 0, 2).reshape(256, 8 * W))


def solution(mesh):
    placed = (
        P(("tok", "feat"), None),
        P(("tok", "feat"), None),
        P("tok", "feat"),
        P("feat"),
        P("feat", "tok"),
        P("tok", "feat"),
    )
    return jax.shard_map(
        on_device,
        mesh=mesh,
        in_specs=placed,
        out_specs=(P(("tok", "feat"), None), P(None, "feat"), P("feat"), P("feat", None)),
        check_vma=False,
    )
```

```python
import math

import jax
import jax.numpy as jnp
from jax import lax
from jax.experimental import pallas as pl
from jax.experimental.pallas import tpu as pltpu
from jax.sharding import PartitionSpec as P

BF = jnp.bfloat16
F32 = jnp.float32
W = 448


def kernel(st_ref, enc_ref, bias_ref, dec_ref, act_ref, err_ref, ge_ref, gb_ref, gd_ref,
           st_in, st_rows, S, G, ST, wt, dt, gate, pre, feats, fT, prnd, part, r0, pb, r1, qb, r2, ebuf, ss, rs):
    tok = lax.axis_index("tok")
    feat = lax.axis_index("feat")
    zh, x = tok // 4, tok % 4
    zlo, y, c = feat // 8, (feat // 2) % 4, feat % 2
    z = zh * 8 + zlo
    zq, zr = z // 4, z % 4

    def dev(x_=None, y_=None, z_=None, c_=None):
        x_ = x if x_ is None else x_
        y_ = y if y_ is None else y_
        z_ = z if z_ is None else z_
        c_ = c if c_ is None else c_
        return {"tok": (z_ // 8) * 4 + x_, "feat": ((z_ % 8) * 4 + y_) * 2 + c_}

    def tok_dev(d):
        return {"tok": (tok + d) % 8, "feat": feat}

    zoff = (1, 15, 2)
    zback = (15, 1, 14)

    barrier = pltpu.get_barrier_semaphore()
    greet = [tok_dev(d) for d in range(1, 8)]
    greet += [dev(z_=(z + 4 * d) % 16) for d in (1, 3)]
    greet += [dev(z_=(z + d) % 16) for d in zback]
    greet += [dev(y_=(y + d) % 4) for d in (1, 2, 3)]
    greet += [dev(c_=1 - c)]
    greet += [dev(z_=zh * 8 + (zlo + d) % 8) for d in range(1, 8)]
    for g in greet:
        pl.semaphore_signal(barrier, inc=1, device_id=g, device_id_type=pl.DeviceIdType.MESH)

    nxt = [0]
    sent = []

    def send(src, dst, to):
        i = nxt[0]
        nxt[0] += 1
        cp = pltpu.make_async_remote_copy(
            src_ref=src, dst_ref=dst, send_sem=ss.at[i], recv_sem=rs.at[i],
            device_id=to, device_id_type=pl.DeviceIdType.MESH)
        cp.start()
        sent.append(cp)
        return cp

    def arrive(cps):
        for cp in cps:
            cp.wait_recv()

    me = x * 2 + zh
    wt[me, 0:W, :] = enc_ref[...]
    wt[me, W:W + 128, :] = act_ref[...].astype(F32).astype(BF)
    dt[me] = dec_ref[...]
    pl.semaphore_wait(barrier, len(greet))

    ex = [send(st_ref.at[(tok + d) % 8], st_in.at[tok], tok_dev(d)) for d in range(1, 8)]
    wz = send(wt.at[me], wt.at[me], dev(z_=(z + 8) % 16))
    st_in[tok] = st_ref[tok]
    arrive(ex)
    for k in range(8):
        v = st_in[k]
        st_rows[0, 2 * k:2 * k + 2, :] = v[0:2]
        st_rows[1, 2 * k:2 * k + 2, :] = v[2:4]

    base = ((c * 4 + y) * 4 + x) * 4

    def ring_start(piece, axis):
        p = {"x_": x, "y_": y}[axis]
        fwd, bwd = dev(**{axis: (p + 1) % 4}), dev(**{axis: (p + 3) % 4})
        own = [piece(p, 0), piece(p, 1)]
        a = send(own[0], own[0], fwd)
        b = send(own[1], own[1], bwd)
        late = [send(own[1], own[1], fwd), send(own[0], own[0], bwd)]
        return piece, p, fwd, bwd, a, b, late

    def ring_pass(state):
        piece, p, fwd, bwd, a, b, late = state
        arrive([a])
        left = piece((p + 3) % 4, 0)
        f = send(left, left, fwd)
        arrive([b])
        right = piece((p + 1) % 4, 1)
        g = send(right, right, bwd)
        return late, [f, g]

    def s_piece(yy, half):
        return S.at[pl.ds((c * 4 + yy) * 16 + half * 8, 8)]

    def w_piece(buf):
        return lambda xx, half: buf.at[2 * xx + half]

    own = base + zq
    S[own, zr] = st_rows[0].astype(BF)
    arrive([send(S.at[own, zr], S.at[own, zr], dev(z_=(z + 4 * d) % 16)) for d in (2, 1, 3)])
    col = S.at[pl.ds(base, 4), zr]
    arrive([send(col, col, dev(z_=(z + d) % 16)) for d in zoff])
    blk = S.at[pl.ds(base, 4)]
    sx = [send(blk, blk, dev(x_=(x + d) % 4)) for d in (1, 3, 2)]
    arrive([wz])
    wx = ring_start(w_piece(wt), "x_")
    dz = send(dt.at[me], dt.at[me], dev(z_=(z + 8) % 16))
    arrive(sx)
    sy = ring_start(s_piece, "y_")

    def s_swap(yy):
        q = S.at[pl.ds((c * 4 + yy) * 16, 16)]
        return send(q, q, dev(c_=1 - c))

    sc = [s_swap(y)]
    wl, wf = ring_pass(wx)
    sl, sf = ring_pass(sy)
    arrive(wl)
    arrive(wf)

    for h in range(2):
        n = lax.broadcasted_iota(jnp.int32, (512, 128), 0)
        m = lax.broadcasted_iota(jnp.int32, (512, 128), 1)
        fidx = (((n // 16) % 8) * 4 + n // 128) * 2 + h
        want = fidx * 2 + n % 2
        tn = (n // 2) % 8
        acc = jnp.zeros((512, 256), F32)
        for t in range(8):
            perm = jnp.where((m == want) & (tn == t), 1.0, 0.0).astype(BF)
            acc += jnp.dot(perm, wt[(t % 4) * 2 + t // 4, W:W + 128, :], preferred_element_type=F32)
        gate[h] = acc

    def rows(h, k):
        return jnp.concatenate(
            [S[pl.ds(((h * 4 + yy) * 4 + k // 2) * 4 + (k % 2) * 2, 2)].reshape(128, W) for yy in range(4)],
            axis=0)

    def g_rows(h, k):
        parts = []
        for yy in range(4):
            parts.append(G[0, ((h * 4 + yy) * 4 + k // 2) * 2 + k % 2].reshape(64, W))
            parts.append(G[1, ((h * 4 + k // 2) * 4 + yy) * 2 + k % 2].reshape(64, W))
        return jnp.concatenate(parts, axis=0)

    def encode(h):
        pre[...] = jnp.zeros((512, 256), F32)

        def step(k, _):
            pre[...] += jnp.dot(rows(h, k), wt[k, 0:W, :], preferred_element_type=F32)
            return 0

        lax.fori_loop(0, 8, step, 0)
        feats[h] = (gate[h] * (pre[...] + bias_ref[...])).astype(BF)

    def decode(h):
        r = lax.dot_general(feats[h], dt[me], (((1,), (1,)), ((), ())), preferred_element_type=F32)
        part[h] = r.reshape(4, 8, 16, W)

    arrive(sl)
    sc += [s_swap((y + 1) % 4), s_swap((y + 3) % 4)]
    arrive(sf)
    sc.append(s_swap((y + 2) % 4))
    encode(c)
    arrive(sc)
    encode(1 - c)
    decode(1 - c)
    pc = [send(part.at[1 - c, (y + d) % 4], r0.at[(y + d) % 4], dev(c_=1 - c)) for d in (2, 1, 3, 0)]
    decode(c)
    arrive([dz])
    dx = ring_start(w_piece(dt), "x_")
    py = []
    for i, d in enumerate((2, 1, 3)):
        yy = (y + d) % 4
        arrive([pc[i]])
        pb[yy] = (part[c, yy] + r0[yy]).astype(BF)
        py.append(send(pb.at[yy], r1.at[d], dev(y_=yy)))
    arrive([pc[3]])
    for h in range(2):
        fT[h] = feats[h].T
    arrive(py)
    total = part[c, y] + r0[y] + r1[1].astype(F32) + r1[2].astype(F32) + r1[3].astype(F32)
    part[c, y] = total
    qb[...] = total.astype(BF)
    pz = [send(qb.at[(zlo + d) % 8], r2.at[d], dev(z_=zh * 8 + (zlo + d) % 8)) for d in (4, 3, 5, 2, 6, 1, 7)]
    dl, df = ring_pass(dx)
    arrive(pz)
    recon = part[c, y, zlo]
    for d in range(1, 8):
        recon = recon + r2[d].astype(F32)
    err = recon - st_rows[1]

    zl = zq % 2
    b0 = ((c * 4 + y) * 4 + x) * 2
    b1 = ((c * 4 + x) * 4 + y) * 2
    gi = b0 + zl * (b1 - b0) + zh
    G[zl, gi, zr] = (err * (1.0 / 32.0)).astype(BF)
    gown = G.at[zl, gi, zr]
    gz = [send(gown, gown, dev(z_=(z + 4 * d) % 16)) for d in (2, 1, 3)]
    for k in range(8):
        ebuf[k] = err[2 * k:2 * k + 2]
    err_ref[tok] = ebuf[tok]
    eo = [send(ebuf.at[(tok + d) % 8], err_ref.at[tok], tok_dev(d)) for d in range(1, 8)]
    arrive(gz)
    cols = [G.at[0, pl.ds(b0, 2), zr], G.at[1, pl.ds(b1, 2), zr]]
    arrive([send(q, q, dev(z_=(z + d) % 16)) for d in zoff for q in cols])
    g0, g1 = G.at[0, pl.ds(b0, 2)], G.at[1, pl.ds(b1, 2)]
    one = []
    for d in (1, 3, 2):
        one.append(send(g0, g0, dev(x_=(x + d) % 4)))
        one.append(send(g1, g1, dev(y_=(y + d) % 4)))
    arrive(one)

    def g_piece(half_no):
        return lambda p, half: G.at[half_no, pl.ds((c * 4 + p) * 8 + half * 4, 4)]

    def g_swap(half_no, p):
        q = G.at[half_no, pl.ds((c * 4 + p) * 8, 8)]
        return send(q, q, dev(c_=1 - c))

    ra = ring_start(g_piece(0), "y_")
    rb = ring_start(g_piece(1), "x_")
    gc = [g_swap(0, y), g_swap(1, x)]

    def turn(k, _):
        ST[k] = jnp.concatenate([rows(0, k), rows(1, k)], axis=0).T
        return 0

    lax.fori_loop(0, 4, turn, 0)
    al, af = ring_pass(ra)
    bl, bf = ring_pass(rb)
    arrive(dl)
    arrive(df)
    arrive(al)
    arrive(bl)
    gc += [g_swap(0, (y + 1) % 4), g_swap(0, (y + 3) % 4), g_swap(1, (x + 1) % 4), g_swap(1, (x + 3) % 4)]
    lax.fori_loop(4, 8, turn, 0)
    arrive(af)
    gc.append(g_swap(0, (y + 2) % 4))
    arrive(bf)
    gc.append(g_swap(1, (x + 2) % 4))

    def back(h):
        pre[...] = jnp.zeros((512, 256), F32)

        def step(k, _):
            pre[...] += jnp.dot(g_rows(h, k), dt[k], preferred_element_type=F32)
            return 0

        lax.fori_loop(0, 8, step, 0)
        g = gate[h] * pre[...]
        prnd[h] = g.astype(BF)
        return jnp.sum(g, axis=0, keepdims=True)

    bsum = back(c)
    arrive(gc)
    gb_ref[...] = bsum + back(1 - c)

    def grads(n, _):
        halves = []
        for odd in range(2):
            t = 2 * n + odd
            k = (t % 4) * 2 + t // 4
            ge = jnp.zeros((W, 256), F32)
            gd = jnp.zeros((256, W), F32)
            for h in range(2):
                ge += jnp.dot(ST[k, :, h * 512:h * 512 + 512], prnd[h], preferred_element_type=F32)
                gd += jnp.dot(fT[h], g_rows(h, k), preferred_element_type=F32)
            ge_ref[pl.ds(pl.multiple_of(t * W, W), W), :] = ge.astype(BF)
            halves.append(gd)
        both = jnp.concatenate(halves, axis=1).astype(BF)
        gd_ref[:, pl.ds(pl.multiple_of(n * 2 * W, 2 * W), 2 * W)] = both
        return 0

    lax.fori_loop(0, 4, grads, 0)
    arrive(eo)
    for cp in sent:
        cp.wait_send()


def on_device(source, target, enc_weight, enc_bias, dec_weight, active):
    st = jnp.concatenate([source, target], axis=0).astype(F32)
    st = st.reshape(4, 8, W).transpose(1, 0, 2)
    vm = pl.BlockSpec(memory_space=pltpu.VMEM)
    err, ge, gb, gd = pl.pallas_call(
        kernel,
        out_shape=(
            jax.ShapeDtypeStruct((8, 2, W), F32),
            jax.ShapeDtypeStruct((8 * W, 256), BF),
            jax.ShapeDtypeStruct((1, 256), F32),
            jax.ShapeDtypeStruct((256, 8 * W), BF),
        ),
        in_specs=[vm] * 5,
        out_specs=[vm] * 4,
        scratch_shapes=[
            pltpu.VMEM((8, 4, W), F32),
            pltpu.VMEM((2, 16, W), F32),
            pltpu.VMEM((128, 4, 16, W), BF),
            pltpu.VMEM((2, 64, 4, 16, W), BF),
            pltpu.VMEM((8, W, 1024), BF),
            pltpu.VMEM((8, W + 128, 256), BF),
            pltpu.VMEM((8, W, 256), BF),
            pltpu.VMEM((2, 512, 256), F32),
            pltpu.VMEM((512, 256), F32),
            pltpu.VMEM((2, 512, 256), BF),
            pltpu.VMEM((2, 256, 512), BF),
            pltpu.VMEM((2, 512, 256), BF),
            pltpu.VMEM((2, 4, 8, 16, W), F32),
            pltpu.VMEM((4, 8, 16, W), F32),
            pltpu.VMEM((4, 8, 16, W), BF),
            pltpu.VMEM((4, 8, 16, W), BF),
            pltpu.VMEM((8, 16, W), BF),
            pltpu.VMEM((8, 16, W), BF),
            pltpu.VMEM((8, 2, W), F32),
            pltpu.SemaphoreType.DMA((128,)),
            pltpu.SemaphoreType.DMA((128,)),
        ],
        compiler_params=pltpu.CompilerParams(
            collective_id=0, has_side_effects=True, vmem_limit_bytes=56 * 1024 * 1024),
    )(st, enc_weight, enc_bias.reshape(1, 256), dec_weight.T, active)
    err = err.transpose(1, 0, 2).reshape(2, 8 * W)
    return (err, ge, gb.reshape(256), gd)


def solution(mesh):
    placed = (
        P(("tok", "feat"), None),
        P(("tok", "feat"), None),
        P("tok", "feat"),
        P("feat"),
        P("feat", "tok"),
        P("tok", "feat"),
    )
    return jax.shard_map(
        on_device,
        mesh=mesh,
        in_specs=placed,
        out_specs=(P(("tok", "feat"), None), P(None, "feat"), P("feat"), P("feat", None)),
        check_vma=False,
    )
```

```python
import math

import jax
import jax.numpy as jnp
from jax import lax
from jax.experimental import pallas as pl
from jax.experimental.pallas import tpu as pltpu
from jax.sharding import PartitionSpec as P

BF = jnp.bfloat16
F32 = jnp.float32
W = 448


def kernel(src_ref, tgt_ref, enc_ref, bias_ref, dec_ref, act_ref, err_ref, ge_ref, gb_ref, gd_ref,
           st_ref, st_in, st_rows, err_in, S, G, ST, at, wt, dt, gate, pre, feats, fT, prnd, part, r0, pb, r1, qb, r2, ebuf, ss, rs):
    tok = lax.axis_index("tok")
    feat = lax.axis_index("feat")
    zh, x = tok // 4, tok % 4
    zlo, y, c = feat // 8, (feat // 2) % 4, feat % 2
    z = zh * 8 + zlo
    zq, zr = z // 4, z % 4

    def dev(x_=None, y_=None, z_=None, c_=None):
        x_ = x if x_ is None else x_
        y_ = y if y_ is None else y_
        z_ = z if z_ is None else z_
        c_ = c if c_ is None else c_
        return {"tok": (z_ // 8) * 4 + x_, "feat": ((z_ % 8) * 4 + y_) * 2 + c_}

    def tok_dev(d):
        return {"tok": (tok + d) % 8, "feat": feat}

    zoff = (1, 15, 2)
    zback = (15, 1, 14)

    barrier = pltpu.get_barrier_semaphore()
    greet = [tok_dev(d) for d in range(1, 8)]
    greet += [dev(z_=(z + 4 * d) % 16) for d in (1, 3)]
    greet += [dev(z_=(z + d) % 16) for d in zback]
    greet += [dev(y_=(y + d) % 4) for d in (1, 2, 3)]
    greet += [dev(c_=1 - c)]
    greet += [dev(z_=zh * 8 + (zlo + d) % 8) for d in range(1, 8)]
    for g in greet:
        pl.semaphore_signal(barrier, inc=1, device_id=g, device_id_type=pl.DeviceIdType.MESH)

    nxt = [0]
    sent = []

    def send(src, dst, to):
        i = nxt[0]
        nxt[0] += 1
        cp = pltpu.make_async_remote_copy(
            src_ref=src, dst_ref=dst, send_sem=ss.at[i], recv_sem=rs.at[i],
            device_id=to, device_id_type=pl.DeviceIdType.MESH)
        cp.start()
        sent.append(cp)
        return cp

    def arrive(cps):
        for cp in cps:
            cp.wait_recv()

    me = x * 2 + zh
    across = dev(z_=(z + 8) % 16)
    wt[me] = enc_ref[...]
    at[me] = act_ref[...].astype(F32).astype(BF)
    dt[me] = dec_ref[...]
    rows_in = jnp.concatenate([src_ref[...].astype(F32), tgt_ref[...].astype(F32)], axis=0)
    for k in range(8):
        st_ref[k] = rows_in[:, k * W:k * W + W]
    pl.semaphore_wait(barrier, len(greet))

    def ring_start(piece, axis):
        p = {"x_": x, "y_": y}[axis]
        fwd, bwd = dev(**{axis: (p + 1) % 4}), dev(**{axis: (p + 3) % 4})
        own = [piece(p, 0), piece(p, 1)]
        a = send(own[0], own[0], fwd)
        b = send(own[1], own[1], bwd)
        late = [send(own[1], own[1], fwd), send(own[0], own[0], bwd)]
        return piece, p, fwd, bwd, a, b, late

    def ring_pass(state):
        piece, p, fwd, bwd, a, b, late = state
        arrive([a])
        left = piece((p + 3) % 4, 0)
        f = send(left, left, fwd)
        arrive([b])
        right = piece((p + 1) % 4, 1)
        g = send(right, right, bwd)
        return late, [f, g]

    def w_piece(buf, side):
        return lambda xx, half: buf.at[2 * xx + side, pl.ds(half * (W // 2), W // 2)]

    zl = zq % 2
    b0 = ((c * 4 + y) * 4 + x) * 2
    b1 = ((c * 4 + x) * 4 + y) * 2
    gi = b0 + zl * (b1 - b0) + zh

    def far(buf):
        own = buf.at[zl, gi, zr]
        return [send(own, own, dev(z_=(z + 4 * d) % 16)) for d in (2, 1, 3)]

    def near(buf):
        cols = [buf.at[0, pl.ds(b0, 2), zr], buf.at[1, pl.ds(b1, 2), zr]]
        return [send(q, q, dev(z_=(z + d) % 16)) for d in zoff for q in cols]

    def light(buf):
        q0, q1 = buf.at[0, pl.ds(b0, 2)], buf.at[1, pl.ds(b1, 2)]
        out = []
        for d in (1, 3, 2):
            out.append(send(q0, q0, dev(x_=(x + d) % 4)))
            out.append(send(q1, q1, dev(y_=(y + d) % 4)))
        return out

    def heavy(buf, half_no):
        return lambda p, half: buf.at[half_no, pl.ds((c * 4 + p) * 8 + half * 4, 4)]

    def swap(buf, half_no, p):
        q = buf.at[half_no, pl.ds((c * 4 + p) * 8, 8)]
        return send(q, q, dev(c_=1 - c))

    ex = [send(st_ref.at[(tok + d) % 8], st_in.at[tok], tok_dev(d)) for d in range(1, 8)]
    az = send(at.at[me], at.at[me], across)
    w0 = ring_start(w_piece(wt, zh), "x_")

    def w_part(i):
        q = wt.at[me, pl.ds(i * (W // 4), W // 4)]
        return send(q, q, across)

    st_in[tok] = st_ref[tok]
    arrive(ex)
    for k in range(8):
        v = st_in[k]
        st_rows[0, 2 * k:2 * k + 2, :] = v[0:2]
        st_rows[1, 2 * k:2 * k + 2, :] = v[2:4]
    S[zl, gi, zr] = st_rows[0].astype(BF)
    sz = far(S)
    wz = [w_part(0)]
    arrive(sz)
    sn = near(S)
    w0l, w0f = ring_pass(w0)
    arrive(sn)
    one = light(S)
    wz += [w_part(1), w_part(2), w_part(3)]
    arrive([az])
    apair = at.at[pl.ds(2 * x, 2)]
    ax = [send(apair, apair, dev(x_=(x + d) % 4)) for d in (1, 3, 2)]
    arrive(one)
    ra = ring_start(heavy(S, 0), "y_")
    rb = ring_start(heavy(S, 1), "x_")
    sc = [swap(S, 0, y), swap(S, 1, x)]
    arrive(w0l)
    arrive(w0f)
    al, af = ring_pass(ra)
    bl, bf = ring_pass(rb)
    arrive(wz)
    w1 = ring_start(w_piece(wt, 1 - zh), "x_")
    dz = send(dt.at[me], dt.at[me], across)
    arrive(ax)

    for h in range(2):
        n = lax.broadcasted_iota(jnp.int32, (512, 128), 0)
        m = lax.broadcasted_iota(jnp.int32, (512, 128), 1)
        fidx = (((n // 16) % 8) * 4 + n // 128) * 2 + h
        want = fidx * 2 + n % 2
        tn = (n // 2) % 8
        acc = jnp.zeros((512, 256), F32)
        for t in range(8):
            perm = jnp.where((m == want) & (tn == t), 1.0, 0.0).astype(BF)
            acc += jnp.dot(perm, at[(t % 4) * 2 + t // 4], preferred_element_type=F32)
        gate[h] = acc

    w1l, w1f = ring_pass(w1)
    d0 = ring_start(w_piece(dt, zh), "x_")

    def rows(buf, h, k):
        parts = []
        for yy in range(4):
            parts.append(buf[0, ((h * 4 + yy) * 4 + k // 2) * 2 + k % 2].reshape(64, W))
            parts.append(buf[1, ((h * 4 + k // 2) * 4 + yy) * 2 + k % 2].reshape(64, W))
        return jnp.concatenate(parts, axis=0)

    def encode(h):
        pre[...] = jnp.zeros((512, 256), F32)

        def step(k, _):
            pre[...] += jnp.dot(rows(S, h, k), wt[k], preferred_element_type=F32)
            return 0

        lax.fori_loop(0, 8, step, 0)
        feats[h] = (gate[h] * (pre[...] + bias_ref[...])).astype(BF)

    def decode(h):
        r = lax.dot_general(feats[h], dt[me], (((1,), (1,)), ((), ())), preferred_element_type=F32)
        part[h] = r.reshape(4, 8, 16, W)

    arrive(al)
    arrive(bl)
    sc += [swap(S, 0, (y + 1) % 4), swap(S, 0, (y + 3) % 4), swap(S, 1, (x + 1) % 4), swap(S, 1, (x + 3) % 4)]
    arrive(af)
    sc.append(swap(S, 0, (y + 2) % 4))
    arrive(bf)
    sc.append(swap(S, 1, (x + 2) % 4))
    arrive(w1l)
    arrive(w1f)
    encode(c)
    d0l, d0f = ring_pass(d0)
    arrive(sc)
    encode(1 - c)
    decode(1 - c)
    pc = [send(part.at[1 - c, (y + d) % 4], r0.at[(y + d) % 4], dev(c_=1 - c)) for d in (2, 1, 3, 0)]
    decode(c)
    arrive([dz])
    d1 = ring_start(w_piece(dt, 1 - zh), "x_")
    py = []
    for i, d in enumerate((2, 1, 3)):
        yy = (y + d) % 4
        arrive([pc[i]])
        pb[yy] = (part[c, yy] + r0[yy]).astype(BF)
        py.append(send(pb.at[yy], r1.at[d], dev(y_=yy)))
    arrive([pc[3]])
    for h in range(2):
        fT[h] = feats[h].T
    arrive(py)
    total = part[c, y] + r0[y] + r1[1].astype(F32) + r1[2].astype(F32) + r1[3].astype(F32)
    part[c, y] = total
    qb[...] = total.astype(BF)
    pz = [send(qb.at[(zlo + d) % 8], r2.at[d], dev(z_=zh * 8 + (zlo + d) % 8)) for d in (4, 3, 5, 2, 6, 1, 7)]
    d1l, d1f = ring_pass(d1)
    arrive(pz)
    recon = part[c, y, zlo]
    for d in range(1, 8):
        recon = recon + r2[d].astype(F32)
    err = recon - st_rows[1]

    G[zl, gi, zr] = (err * (1.0 / 32.0)).astype(BF)
    gz = far(G)
    for k in range(8):
        ebuf[k] = err[2 * k:2 * k + 2]
    err_in[tok] = ebuf[tok]
    eo = [send(ebuf.at[(tok + d) % 8], err_in.at[tok], tok_dev(d)) for d in range(1, 8)]
    arrive(gz)
    arrive(near(G))
    arrive(light(G))
    ra = ring_start(heavy(G, 0), "y_")
    rb = ring_start(heavy(G, 1), "x_")
    gc = [swap(G, 0, y), swap(G, 1, x)]

    def turn(k, _):
        ST[k] = jnp.concatenate([rows(S, 0, k), rows(S, 1, k)], axis=0).T
        return 0

    lax.fori_loop(0, 4, turn, 0)
    al, af = ring_pass(ra)
    bl, bf = ring_pass(rb)
    for cps in (d0l, d0f, d1l, d1f):
        arrive(cps)
    arrive(al)
    arrive(bl)
    gc += [swap(G, 0, (y + 1) % 4), swap(G, 0, (y + 3) % 4), swap(G, 1, (x + 1) % 4), swap(G, 1, (x + 3) % 4)]
    lax.fori_loop(4, 8, turn, 0)
    arrive(af)
    gc.append(swap(G, 0, (y + 2) % 4))
    arrive(bf)
    gc.append(swap(G, 1, (x + 2) % 4))

    def back(h):
        pre[...] = jnp.zeros((512, 256), F32)

        def step(k, _):
            pre[...] += jnp.dot(rows(G, h, k), dt[k], preferred_element_type=F32)
            return 0

        lax.fori_loop(0, 8, step, 0)
        g = gate[h] * pre[...]
        prnd[h] = g.astype(BF)
        return jnp.sum(g, axis=0, keepdims=True)

    bsum = back(c)
    arrive(gc)
    gb_ref[...] = bsum + back(1 - c)

    def grads(n, _):
        halves = []
        for odd in range(2):
            t = 2 * n + odd
            k = (t % 4) * 2 + t // 4
            ge = jnp.zeros((W, 256), F32)
            gd = jnp.zeros((256, W), F32)
            for h in range(2):
                ge += jnp.dot(ST[k, :, h * 512:h * 512 + 512], prnd[h], preferred_element_type=F32)
                gd += jnp.dot(fT[h], rows(G, h, k), preferred_element_type=F32)
            ge_ref[pl.ds(pl.multiple_of(t * W, W), W), :] = ge.astype(BF)
            halves.append(gd)
        both = jnp.concatenate(halves, axis=1).astype(BF)
        gd_ref[:, pl.ds(pl.multiple_of(n * 2 * W, 2 * W), 2 * W)] = both
        return 0

    arrive(eo)
    err_ref[...] = jnp.concatenate([err_in[k] for k in range(8)], axis=1)
    lax.fori_loop(0, 4, grads, 0)
    for cp in sent:
        cp.wait_send()


def on_device(source, target, enc_weight, enc_bias, dec_weight, active):
    vm = pl.BlockSpec(memory_space=pltpu.VMEM)
    err, ge, gb, gd = pl.pallas_call(
        kernel,
        out_shape=(
            jax.ShapeDtypeStruct((2, 8 * W), F32),
            jax.ShapeDtypeStruct((8 * W, 256), BF),
            jax.ShapeDtypeStruct((1, 256), F32),
            jax.ShapeDtypeStruct((256, 8 * W), BF),
        ),
        in_specs=[vm] * 6,
        out_specs=[vm] * 4,
        scratch_shapes=[
            pltpu.VMEM((8, 4, W), F32),
            pltpu.VMEM((8, 4, W), F32),
            pltpu.VMEM((2, 16, W), F32),
            pltpu.VMEM((8, 2, W), F32),
            pltpu.VMEM((2, 64, 4, 16, W), BF),
            pltpu.VMEM((2, 64, 4, 16, W), BF),
            pltpu.VMEM((8, W, 1024), BF),
            pltpu.VMEM((8, 128, 256), BF),
            pltpu.VMEM((8, W, 256), BF),
            pltpu.VMEM((8, W, 256), BF),
            pltpu.VMEM((2, 512, 256), F32),
            pltpu.VMEM((512, 256), F32),
            pltpu.VMEM((2, 512, 256), BF),
            pltpu.VMEM((2, 256, 512), BF),
            pltpu.VMEM((2, 512, 256), BF),
            pltpu.VMEM((2, 4, 8, 16, W), F32),
            pltpu.VMEM((4, 8, 16, W), F32),
            pltpu.VMEM((4, 8, 16, W), BF),
            pltpu.VMEM((4, 8, 16, W), BF),
            pltpu.VMEM((8, 16, W), BF),
            pltpu.VMEM((8, 16, W), BF),
            pltpu.VMEM((8, 2, W), F32),
            pltpu.SemaphoreType.DMA((144,)),
            pltpu.SemaphoreType.DMA((144,)),
        ],
        compiler_params=pltpu.CompilerParams(
            collective_id=0, has_side_effects=True, vmem_limit_bytes=56 * 1024 * 1024),
    )(source, target, enc_weight, enc_bias.reshape(1, 256), dec_weight.T, active)
    return (err, ge, gb.reshape(256), gd)


def solution(mesh):
    placed = (
        P(("tok", "feat"), None),
        P(("tok", "feat"), None),
        P("tok", "feat"),
        P("feat"),
        P("feat", "tok"),
        P("tok", "feat"),
    )
    return jax.shard_map(
        on_device,
        mesh=mesh,
        in_specs=placed,
        out_specs=(P(("tok", "feat"), None), P(None, "feat"), P("feat"), P("feat", None)),
        check_vma=False,
    )
```

```python
import math

import jax
import jax.numpy as jnp
from jax import lax
from jax.experimental import pallas as pl
from jax.experimental.pallas import tpu as pltpu
from jax.sharding import PartitionSpec as P

BF = jnp.bfloat16
F32 = jnp.float32
W = 448


def kernel(src_ref, tgt_ref, enc_ref, bias_ref, dec_ref, act_ref, err_ref, ge_ref, gb_ref, gd_ref,
           st_ref, st_in, st_rows, err_in, S, G, ST, at, wt, dt, gate, pre, feats, fT, prnd, part, r0, pb, r1, qb, r2, ebuf, ss, rs):
    tok = lax.axis_index("tok")
    feat = lax.axis_index("feat")
    zh, x = tok // 4, tok % 4
    zlo, y, c = feat // 8, (feat // 2) % 4, feat % 2
    z = zh * 8 + zlo
    zq, zr = z // 4, z % 4

    def dev(x_=None, y_=None, z_=None, c_=None):
        x_ = x if x_ is None else x_
        y_ = y if y_ is None else y_
        z_ = z if z_ is None else z_
        c_ = c if c_ is None else c_
        return {"tok": (z_ // 8) * 4 + x_, "feat": ((z_ % 8) * 4 + y_) * 2 + c_}

    def tok_dev(d):
        return {"tok": (tok + d) % 8, "feat": feat}

    zoff = (1, 15, 2)
    zback = (15, 1, 14)

    barrier = pltpu.get_barrier_semaphore()
    greet = [tok_dev(d) for d in range(1, 8)]
    greet += [dev(z_=(z + 4 * d) % 16) for d in (1, 3)]
    greet += [dev(z_=(z + d) % 16) for d in zback]
    greet += [dev(y_=(y + d) % 4) for d in (1, 2, 3)]
    greet += [dev(c_=1 - c)]
    greet += [dev(z_=zh * 8 + (zlo + d) % 8) for d in range(1, 8)]
    for g in greet:
        pl.semaphore_signal(barrier, inc=1, device_id=g, device_id_type=pl.DeviceIdType.MESH)

    nxt = [0]
    sent = []

    def send(src, dst, to):
        i = nxt[0]
        nxt[0] += 1
        cp = pltpu.make_async_remote_copy(
            src_ref=src, dst_ref=dst, send_sem=ss.at[i], recv_sem=rs.at[i],
            device_id=to, device_id_type=pl.DeviceIdType.MESH)
        cp.start()
        sent.append(cp)
        return cp

    def arrive(cps):
        for cp in cps:
            cp.wait_recv()

    me = x * 2 + zh
    across = dev(z_=(z + 8) % 16)
    wt[me] = enc_ref[...]
    at[me] = act_ref[...].astype(F32).astype(BF)
    dt[me] = dec_ref[...]
    rows_in = jnp.concatenate([src_ref[...].astype(F32), tgt_ref[...].astype(F32)], axis=0)
    for k in range(8):
        st_ref[k] = rows_in[:, k * W:k * W + W]
    pl.semaphore_wait(barrier, len(greet))

    def ring_start(piece, axis):
        p = {"x_": x, "y_": y}[axis]
        fwd, bwd = dev(**{axis: (p + 1) % 4}), dev(**{axis: (p + 3) % 4})
        own = [piece(p, 0), piece(p, 1)]
        a = send(own[0], own[0], fwd)
        b = send(own[1], own[1], bwd)
        late = [send(own[1], own[1], fwd), send(own[0], own[0], bwd)]
        return piece, p, fwd, bwd, a, b, late

    def ring_pass(state):
        piece, p, fwd, bwd, a, b, late = state
        arrive([a])
        left = piece((p + 3) % 4, 0)
        f = send(left, left, fwd)
        arrive([b])
        right = piece((p + 1) % 4, 1)
        g = send(right, right, bwd)
        return late, [f, g]

    def w_piece(buf, side):
        return lambda xx, half: buf.at[2 * xx + side, pl.ds(half * (W // 2), W // 2)]

    zl = zq % 2
    b0 = ((c * 4 + y) * 4 + x) * 2
    b1 = ((c * 4 + x) * 4 + y) * 2
    gi = b0 + zl * (b1 - b0) + zh

    def far(buf):
        own = buf.at[zl, gi, zr]
        return [send(own, own, dev(z_=(z + 4 * d) % 16)) for d in (2, 1, 3)]

    def near(buf):
        cols = [buf.at[0, pl.ds(b0, 2), zr], buf.at[1, pl.ds(b1, 2), zr]]
        return [send(q, q, dev(z_=(z + d) % 16)) for d in zoff for q in cols]

    def light(buf):
        q0, q1 = buf.at[0, pl.ds(b0, 2)], buf.at[1, pl.ds(b1, 2)]
        out = []
        for d in (1, 3, 2):
            out.append(send(q0, q0, dev(x_=(x + d) % 4)))
            out.append(send(q1, q1, dev(y_=(y + d) % 4)))
        return out

    def heavy(buf, half_no):
        return lambda p, half: buf.at[half_no, pl.ds((c * 4 + p) * 8 + half * 4, 4)]

    def swap(buf, half_no, p):
        q = buf.at[half_no, pl.ds((c * 4 + p) * 8, 8)]
        return send(q, q, dev(c_=1 - c))

    ex = [send(st_ref.at[(tok + d) % 8], st_in.at[tok], tok_dev(d)) for d in range(1, 8)]
    az = send(at.at[me], at.at[me], across)
    w0 = ring_start(w_piece(wt, zh), "x_")

    def w_part(i):
        q = wt.at[me, pl.ds(i * (W // 4), W // 4)]
        return send(q, q, across)

    st_in[tok] = st_ref[tok]
    arrive(ex)
    for k in range(8):
        v = st_in[k]
        st_rows[0, 2 * k:2 * k + 2, :] = v[0:2]
        st_rows[1, 2 * k:2 * k + 2, :] = v[2:4]
    S[zl, gi, zr] = st_rows[0].astype(BF)
    sz = far(S)
    wz = [w_part(0), w_part(1)]
    arrive(sz)
    sn = near(S)
    w0l, w0f = ring_pass(w0)
    arrive(sn)
    one = light(S)
    wz += [w_part(2), w_part(3)]
    arrive([az])
    apair = at.at[pl.ds(2 * x, 2)]
    ax = [send(apair, apair, dev(x_=(x + d) % 4)) for d in (1, 3, 2)]
    arrive(one)
    ra = ring_start(heavy(S, 0), "y_")
    rb = ring_start(heavy(S, 1), "x_")
    sc = [swap(S, 0, y), swap(S, 1, x)]
    arrive(w0l)
    arrive(w0f)
    al, af = ring_pass(ra)
    bl, bf = ring_pass(rb)
    arrive(ax)

    for h in range(2):
        n = lax.broadcasted_iota(jnp.int32, (512, 128), 0)
        m = lax.broadcasted_iota(jnp.int32, (512, 128), 1)
        fidx = (((n // 16) % 8) * 4 + n // 128) * 2 + h
        want = fidx * 2 + n % 2
        tn = (n // 2) % 8
        acc = jnp.zeros((512, 256), F32)
        for t in range(8):
            perm = jnp.where((m == want) & (tn == t), 1.0, 0.0).astype(BF)
            acc += jnp.dot(perm, at[(t % 4) * 2 + t // 4], preferred_element_type=F32)
        gate[h] = acc

    dz = send(dt.at[me], dt.at[me], across)
    arrive(wz)
    w1 = ring_start(w_piece(wt, 1 - zh), "x_")

    def rows(buf, h, k):
        parts = []
        for yy in range(4):
            parts.append(buf[0, ((h * 4 + yy) * 4 + k // 2) * 2 + k % 2].reshape(64, W))
            parts.append(buf[1, ((h * 4 + k // 2) * 4 + yy) * 2 + k % 2].reshape(64, W))
        return jnp.concatenate(parts, axis=0)

    def encode(h, side):
        def step(i, _):
            pre[h] += jnp.dot(rows(S, h, 2 * i + side), wt[2 * i + side], preferred_element_type=F32)
            return 0

        lax.fori_loop(0, 4, step, 0)

    def finish(h):
        feats[h] = (gate[h] * (pre[h] + bias_ref[...])).astype(BF)

    def decode(h):
        r = lax.dot_general(feats[h], dt[me], (((1,), (1,)), ((), ())), preferred_element_type=F32)
        part[h] = r.reshape(4, 8, 16, W)

    arrive(al)
    arrive(bl)
    sc += [swap(S, 0, (y + 1) % 4), swap(S, 0, (y + 3) % 4), swap(S, 1, (x + 1) % 4), swap(S, 1, (x + 3) % 4)]
    arrive(af)
    sc.append(swap(S, 0, (y + 2) % 4))
    arrive(bf)
    sc.append(swap(S, 1, (x + 2) % 4))
    w1l, w1f = ring_pass(w1)
    d0 = ring_start(w_piece(dt, zh), "x_")
    pre[...] = jnp.zeros((2, 512, 256), F32)
    encode(c, zh)
    arrive(sc)
    encode(1 - c, zh)
    arrive(w1l)
    arrive(w1f)
    encode(1 - c, 1 - zh)
    finish(1 - c)
    decode(1 - c)
    pc = [send(part.at[1 - c, (y + d) % 4], r0.at[(y + d) % 4], dev(c_=1 - c)) for d in (2, 1, 3, 0)]
    encode(c, 1 - zh)
    finish(c)
    d0l, d0f = ring_pass(d0)
    decode(c)
    py = []
    for i, d in enumerate((2, 1, 3)):
        yy = (y + d) % 4
        arrive([pc[i]])
        pb[yy] = (part[c, yy] + r0[yy]).astype(BF)
        py.append(send(pb.at[yy], r1.at[d], dev(y_=yy)))
    arrive([pc[3]])
    for h in range(2):
        fT[h] = feats[h].T
    arrive(py)
    total = part[c, y] + r0[y] + r1[1].astype(F32) + r1[2].astype(F32) + r1[3].astype(F32)
    part[c, y] = total
    qb[...] = total.astype(BF)
    pz = [send(qb.at[(zlo + d) % 8], r2.at[d], dev(z_=zh * 8 + (zlo + d) % 8)) for d in (4, 3, 5, 2, 6, 1, 7)]
    arrive([dz])
    d1 = ring_start(w_piece(dt, 1 - zh), "x_")
    arrive(pz)
    recon = part[c, y, zlo]
    for d in range(1, 8):
        recon = recon + r2[d].astype(F32)
    err = recon - st_rows[1]

    G[zl, gi, zr] = (err * (1.0 / 32.0)).astype(BF)
    gz = far(G)
    for k in range(8):
        ebuf[k] = err[2 * k:2 * k + 2]
    err_in[tok] = ebuf[tok]
    eo = [send(ebuf.at[(tok + d) % 8], err_in.at[tok], tok_dev(d)) for d in range(1, 8)]
    d1l, d1f = ring_pass(d1)
    arrive(gz)
    arrive(near(G))
    arrive(light(G))
    ra = ring_start(heavy(G, 0), "y_")
    rb = ring_start(heavy(G, 1), "x_")
    gc = [swap(G, 0, y), swap(G, 1, x)]

    def turn(k, _):
        ST[k] = jnp.concatenate([rows(S, 0, k), rows(S, 1, k)], axis=0).T
        return 0

    lax.fori_loop(0, 4, turn, 0)
    al, af = ring_pass(ra)
    bl, bf = ring_pass(rb)
    for cps in (d0l, d0f, d1l, d1f):
        arrive(cps)
    arrive(al)
    arrive(bl)
    gc += [swap(G, 0, (y + 1) % 4), swap(G, 0, (y + 3) % 4), swap(G, 1, (x + 1) % 4), swap(G, 1, (x + 3) % 4)]
    lax.fori_loop(4, 8, turn, 0)
    arrive(af)
    gc.append(swap(G, 0, (y + 2) % 4))
    arrive(bf)
    gc.append(swap(G, 1, (x + 2) % 4))

    def back(h):
        pre[h] = jnp.zeros((512, 256), F32)

        def step(k, _):
            pre[h] += jnp.dot(rows(G, h, k), dt[k], preferred_element_type=F32)
            return 0

        lax.fori_loop(0, 8, step, 0)
        g = gate[h] * pre[h]
        prnd[h] = g.astype(BF)
        return jnp.sum(g, axis=0, keepdims=True)

    bsum = back(c)
    arrive(gc)
    gb_ref[...] = bsum + back(1 - c)

    def grads(n, _):
        halves = []
        for odd in range(2):
            t = 2 * n + odd
            k = (t % 4) * 2 + t // 4
            ge = jnp.zeros((W, 256), F32)
            gd = jnp.zeros((256, W), F32)
            for h in range(2):
                ge += jnp.dot(ST[k, :, h * 512:h * 512 + 512], prnd[h], preferred_element_type=F32)
                gd += jnp.dot(fT[h], rows(G, h, k), preferred_element_type=F32)
            ge_ref[pl.ds(pl.multiple_of(t * W, W), W), :] = ge.astype(BF)
            halves.append(gd)
        both = jnp.concatenate(halves, axis=1).astype(BF)
        gd_ref[:, pl.ds(pl.multiple_of(n * 2 * W, 2 * W), 2 * W)] = both
        return 0

    arrive(eo)
    err_ref[...] = jnp.concatenate([err_in[k] for k in range(8)], axis=1)
    lax.fori_loop(0, 4, grads, 0)
    for cp in sent:
        cp.wait_send()


def on_device(source, target, enc_weight, enc_bias, dec_weight, active):
    vm = pl.BlockSpec(memory_space=pltpu.VMEM)
    err, ge, gb, gd = pl.pallas_call(
        kernel,
        out_shape=(
            jax.ShapeDtypeStruct((2, 8 * W), F32),
            jax.ShapeDtypeStruct((8 * W, 256), BF),
            jax.ShapeDtypeStruct((1, 256), F32),
            jax.ShapeDtypeStruct((256, 8 * W), BF),
        ),
        in_specs=[vm] * 6,
        out_specs=[vm] * 4,
        scratch_shapes=[
            pltpu.VMEM((8, 4, W), F32),
            pltpu.VMEM((8, 4, W), F32),
            pltpu.VMEM((2, 16, W), F32),
            pltpu.VMEM((8, 2, W), F32),
            pltpu.VMEM((2, 64, 4, 16, W), BF),
            pltpu.VMEM((2, 64, 4, 16, W), BF),
            pltpu.VMEM((8, W, 1024), BF),
            pltpu.VMEM((8, 128, 256), BF),
            pltpu.VMEM((8, W, 256), BF),
            pltpu.VMEM((8, W, 256), BF),
            pltpu.VMEM((2, 512, 256), F32),
            pltpu.VMEM((2, 512, 256), F32),
            pltpu.VMEM((2, 512, 256), BF),
            pltpu.VMEM((2, 256, 512), BF),
            pltpu.VMEM((2, 512, 256), BF),
            pltpu.VMEM((2, 4, 8, 16, W), F32),
            pltpu.VMEM((4, 8, 16, W), F32),
            pltpu.VMEM((4, 8, 16, W), BF),
            pltpu.VMEM((4, 8, 16, W), BF),
            pltpu.VMEM((8, 16, W), BF),
            pltpu.VMEM((8, 16, W), BF),
            pltpu.VMEM((8, 2, W), F32),
            pltpu.SemaphoreType.DMA((144,)),
            pltpu.SemaphoreType.DMA((144,)),
        ],
        compiler_params=pltpu.CompilerParams(
            collective_id=0, has_side_effects=True, vmem_limit_bytes=56 * 1024 * 1024),
    )(source, target, enc_weight, enc_bias.reshape(1, 256), dec_weight.T, active)
    return (err, ge, gb.reshape(256), gd)


def solution(mesh):
    placed = (
        P(("tok", "feat"), None),
        P(("tok", "feat"), None),
        P("tok", "feat"),
        P("feat"),
        P("feat", "tok"),
        P("tok", "feat"),
    )
    return jax.shard_map(
        on_device,
        mesh=mesh,
        in_specs=placed,
        out_specs=(P(("tok", "feat"), None), P(None, "feat"), P("feat"), P("feat", None)),
        check_vma=False,
    )
```

```python
import math

import jax
import jax.numpy as jnp
from jax import lax
from jax.experimental import pallas as pl
from jax.experimental.pallas import tpu as pltpu
from jax.sharding import PartitionSpec as P

BF = jnp.bfloat16
F32 = jnp.float32
W = 448


def kernel(src_ref, tgt_ref, enc_ref, bias_ref, dec_ref, act_ref, err_ref, ge_ref, gb_ref, gd_ref,
           st_ref, st_in, st_rows, err_in, S, G, ST, at, wt, dt, gate, pre, feats, fT, prnd, part, r0, pb, r1, qb, r2, ebuf, ss, rs):
    tok = lax.axis_index("tok")
    feat = lax.axis_index("feat")
    zh, x = tok // 4, tok % 4
    zlo, y, c = feat // 8, (feat // 2) % 4, feat % 2
    z = zh * 8 + zlo
    zq, zr = z // 4, z % 4

    def dev(x_=None, y_=None, z_=None, c_=None):
        x_ = x if x_ is None else x_
        y_ = y if y_ is None else y_
        z_ = z if z_ is None else z_
        c_ = c if c_ is None else c_
        return {"tok": (z_ // 8) * 4 + x_, "feat": ((z_ % 8) * 4 + y_) * 2 + c_}

    def tok_dev(d):
        return {"tok": (tok + d) % 8, "feat": feat}

    zoff = (1, 15, 2)
    zback = (15, 1, 14)

    barrier = pltpu.get_barrier_semaphore()
    greet = [tok_dev(d) for d in range(1, 8)]
    greet += [dev(z_=(z + 4 * d) % 16) for d in (1, 3)]
    greet += [dev(z_=(z + d) % 16) for d in zback]
    greet += [dev(y_=(y + d) % 4) for d in (1, 2, 3)]
    greet += [dev(c_=1 - c)]
    greet += [dev(z_=zh * 8 + (zlo + d) % 8) for d in range(1, 8)]
    for g in greet:
        pl.semaphore_signal(barrier, inc=1, device_id=g, device_id_type=pl.DeviceIdType.MESH)

    nxt = [0]
    sent = []

    def send(src, dst, to):
        i = nxt[0]
        nxt[0] += 1
        cp = pltpu.make_async_remote_copy(
            src_ref=src, dst_ref=dst, send_sem=ss.at[i], recv_sem=rs.at[i],
            device_id=to, device_id_type=pl.DeviceIdType.MESH)
        cp.start()
        sent.append(cp)
        return cp

    def arrive(cps):
        for cp in cps:
            cp.wait_recv()

    me = x * 2 + zh
    across = dev(z_=(z + 8) % 16)
    wt[me] = enc_ref[...]
    at[me] = act_ref[...].astype(F32).astype(BF)
    dt[me] = dec_ref[...]
    rows_in = jnp.concatenate([src_ref[...].astype(F32), tgt_ref[...].astype(F32)], axis=0)
    for k in range(8):
        st_ref[k] = rows_in[:, k * W:k * W + W]
    pl.semaphore_wait(barrier, len(greet))

    def ring_start(piece, axis):
        p = {"x_": x, "y_": y}[axis]
        fwd, bwd = dev(**{axis: (p + 1) % 4}), dev(**{axis: (p + 3) % 4})
        own = [piece(p, 0), piece(p, 1)]
        a = send(own[0], own[0], fwd)
        b = send(own[1], own[1], bwd)
        late = [send(own[1], own[1], fwd), send(own[0], own[0], bwd)]
        return piece, p, fwd, bwd, a, b, late

    def ring_pass(state):
        piece, p, fwd, bwd, a, b, late = state
        arrive([a])
        left = piece((p + 3) % 4, 0)
        f = send(left, left, fwd)
        arrive([b])
        right = piece((p + 1) % 4, 1)
        g = send(right, right, bwd)
        return late, [f, g]

    def w_piece(buf, side):
        return lambda xx, half: buf.at[2 * xx + side, pl.ds(half * (W // 2), W // 2)]

    zl = zq % 2
    b0 = ((c * 4 + y) * 4 + x) * 2
    b1 = ((c * 4 + x) * 4 + y) * 2
    gi = b0 + zl * (b1 - b0) + zh

    def far(buf):
        own = buf.at[zl, gi, zr]
        return [send(own, own, dev(z_=(z + 4 * d) % 16)) for d in (2, 1, 3)]

    def near(buf):
        cols = [buf.at[0, pl.ds(b0, 2), zr], buf.at[1, pl.ds(b1, 2), zr]]
        return [send(q, q, dev(z_=(z + d) % 16)) for d in zoff for q in cols]

    def light(buf):
        q0, q1 = buf.at[0, pl.ds(b0, 2)], buf.at[1, pl.ds(b1, 2)]
        out = []
        for d in (1, 3, 2):
            out.append(send(q0, q0, dev(x_=(x + d) % 4)))
            out.append(send(q1, q1, dev(y_=(y + d) % 4)))
        return out

    def heavy(buf, half_no):
        return lambda p, half: buf.at[half_no, pl.ds((c * 4 + p) * 8 + half * 4, 4)]

    def swap(buf, half_no, p):
        q = buf.at[half_no, pl.ds((c * 4 + p) * 8, 8)]
        return send(q, q, dev(c_=1 - c))

    ex = [send(st_ref.at[(tok + d) % 8], st_in.at[tok], tok_dev(d)) for d in range(1, 8)]
    az = send(at.at[me], at.at[me], across)
    w0 = ring_start(w_piece(wt, zh), "x_")

    def w_part(i):
        q = wt.at[me, pl.ds(i * (W // 4), W // 4)]
        return send(q, q, across)

    st_in[tok] = st_ref[tok]
    arrive(ex)
    for k in range(8):
        v = st_in[k]
        st_rows[0, 2 * k:2 * k + 2, :] = v[0:2]
        st_rows[1, 2 * k:2 * k + 2, :] = v[2:4]
    S[zl, gi, zr] = st_rows[0].astype(BF)
    sz = far(S)
    wz = [w_part(0), w_part(1)]
    arrive(sz)
    sn = near(S)
    arrive([az])
    apair = at.at[pl.ds(2 * x, 2)]
    ax = [send(apair, apair, dev(x_=(x + d) % 4)) for d in (1, 3, 2)]
    w0l, w0f = ring_pass(w0)
    arrive(sn)
    one = light(S)
    wz += [w_part(2), w_part(3)]
    arrive(one)
    ra = ring_start(heavy(S, 0), "y_")
    rb = ring_start(heavy(S, 1), "x_")
    sc = [swap(S, 0, y), swap(S, 1, x)]
    arrive(ax)

    def order(h):
        n = lax.broadcasted_iota(jnp.int32, (512, 128), 0)
        m = lax.broadcasted_iota(jnp.int32, (512, 128), 1)
        fidx = ((((n >> 4) & 7) * 4 + (n >> 7)) * 2) + h
        slot = jnp.where(m == fidx * 2 + (n & 1), (n >> 1) & 7, 8)
        acc = jnp.zeros((512, 256), F32)
        for t in range(8):
            perm = jnp.where(slot == t, 1.0, 0.0).astype(BF)
            acc += jnp.dot(perm, at[(t % 4) * 2 + t // 4], preferred_element_type=F32)
        gate[h] = acc

    order(0)
    al, af = ring_pass(ra)
    bl, bf = ring_pass(rb)
    order(1)
    arrive(w0l)
    arrive(w0f)
    dz = send(dt.at[me], dt.at[me], across)
    arrive(wz)
    w1 = ring_start(w_piece(wt, 1 - zh), "x_")

    def rows(buf, h, k):
        parts = []
        for yy in range(4):
            parts.append(buf[0, ((h * 4 + yy) * 4 + k // 2) * 2 + k % 2].reshape(64, W))
            parts.append(buf[1, ((h * 4 + k // 2) * 4 + yy) * 2 + k % 2].reshape(64, W))
        return jnp.concatenate(parts, axis=0)

    def encode(h, side):
        def step(i, _):
            pre[h] += jnp.dot(rows(S, h, 2 * i + side), wt[2 * i + side], preferred_element_type=F32)
            return 0

        lax.fori_loop(0, 4, step, 0)

    def finish(h):
        feats[h] = (gate[h] * (pre[h] + bias_ref[...])).astype(BF)

    def decode(h):
        r = lax.dot_general(feats[h], dt[me], (((1,), (1,)), ((), ())), preferred_element_type=F32)
        part[h] = r.reshape(4, 8, 16, W)

    arrive(al)
    arrive(bl)
    sc += [swap(S, 0, (y + 1) % 4), swap(S, 0, (y + 3) % 4), swap(S, 1, (x + 1) % 4), swap(S, 1, (x + 3) % 4)]
    arrive(af)
    sc.append(swap(S, 0, (y + 2) % 4))
    arrive(bf)
    sc.append(swap(S, 1, (x + 2) % 4))
    w1l, w1f = ring_pass(w1)
    d0 = ring_start(w_piece(dt, zh), "x_")
    pre[...] = jnp.zeros((2, 512, 256), F32)
    encode(c, zh)
    arrive(sc)
    encode(1 - c, zh)
    arrive(w1l)
    arrive(w1f)
    encode(1 - c, 1 - zh)
    finish(1 - c)
    decode(1 - c)
    pc = [send(part.at[1 - c, (y + d) % 4], r0.at[(y + d) % 4], dev(c_=1 - c)) for d in (2, 1, 3, 0)]
    encode(c, 1 - zh)
    finish(c)
    d0l, d0f = ring_pass(d0)
    decode(c)
    py = []
    for i, d in enumerate((2, 1, 3)):
        yy = (y + d) % 4
        arrive([pc[i]])
        pb[yy] = (part[c, yy] + r0[yy]).astype(BF)
        py.append(send(pb.at[yy], r1.at[d], dev(y_=yy)))
    arrive([pc[3]])
    def turn(k, _):
        ST[k] = jnp.concatenate([rows(S, 0, k), rows(S, 1, k)], axis=0).T
        return 0

    for h in range(2):
        fT[h] = feats[h].T
    lax.fori_loop(0, 1, turn, 0)
    arrive(py)
    total = part[c, y] + r0[y] + r1[1].astype(F32) + r1[2].astype(F32) + r1[3].astype(F32)
    part[c, y] = total
    qb[...] = total.astype(BF)
    pz = [send(qb.at[(zlo + d) % 8], r2.at[d], dev(z_=zh * 8 + (zlo + d) % 8)) for d in (4, 3, 5, 2, 6, 1, 7)]
    arrive([dz])
    d1 = ring_start(w_piece(dt, 1 - zh), "x_")
    lax.fori_loop(1, 4, turn, 0)
    arrive(pz)
    recon = part[c, y, zlo]
    for d in range(1, 8):
        recon = recon + r2[d].astype(F32)
    err = recon - st_rows[1]

    G[zl, gi, zr] = (err * (1.0 / 32.0)).astype(BF)
    gz = far(G)
    for k in range(8):
        ebuf[k] = err[2 * k:2 * k + 2]
    err_in[tok] = ebuf[tok]
    eo = [send(ebuf.at[(tok + d) % 8], err_in.at[tok], tok_dev(d)) for d in range(1, 8)]
    d1l, d1f = ring_pass(d1)
    lax.fori_loop(4, 6, turn, 0)
    arrive(gz)
    arrive(near(G))
    arrive(light(G))
    ra = ring_start(heavy(G, 0), "y_")
    rb = ring_start(heavy(G, 1), "x_")
    gc = [swap(G, 0, y), swap(G, 1, x)]

    lax.fori_loop(6, 8, turn, 0)
    al, af = ring_pass(ra)
    bl, bf = ring_pass(rb)
    for cps in (d0l, d0f, d1l, d1f):
        arrive(cps)
    arrive(al)
    arrive(bl)
    gc += [swap(G, 0, (y + 1) % 4), swap(G, 0, (y + 3) % 4), swap(G, 1, (x + 1) % 4), swap(G, 1, (x + 3) % 4)]
    arrive(af)
    gc.append(swap(G, 0, (y + 2) % 4))
    arrive(bf)
    gc.append(swap(G, 1, (x + 2) % 4))

    def back(h):
        pre[h] = jnp.zeros((512, 256), F32)

        def step(k, _):
            pre[h] += jnp.dot(rows(G, h, k), dt[k], preferred_element_type=F32)
            return 0

        lax.fori_loop(0, 8, step, 0)
        g = gate[h] * pre[h]
        prnd[h] = g.astype(BF)
        return jnp.sum(g, axis=0, keepdims=True)

    bsum = back(c)
    arrive(gc)
    gb_ref[...] = bsum + back(1 - c)

    def grads(n, _):
        halves = []
        for odd in range(2):
            t = 2 * n + odd
            k = (t % 4) * 2 + t // 4
            ge = jnp.zeros((W, 256), F32)
            gd = jnp.zeros((256, W), F32)
            for h in range(2):
                ge += jnp.dot(ST[k, :, h * 512:h * 512 + 512], prnd[h], preferred_element_type=F32)
                gd += jnp.dot(fT[h], rows(G, h, k), preferred_element_type=F32)
            ge_ref[pl.ds(pl.multiple_of(t * W, W), W), :] = ge.astype(BF)
            halves.append(gd)
        both = jnp.concatenate(halves, axis=1).astype(BF)
        gd_ref[:, pl.ds(pl.multiple_of(n * 2 * W, 2 * W), 2 * W)] = both
        return 0

    arrive(eo)
    err_ref[...] = jnp.concatenate([err_in[k] for k in range(8)], axis=1)
    lax.fori_loop(0, 4, grads, 0)
    for cp in sent:
        cp.wait_send()


def on_device(source, target, enc_weight, enc_bias, dec_weight, active):
    vm = pl.BlockSpec(memory_space=pltpu.VMEM)
    err, ge, gb, gd = pl.pallas_call(
        kernel,
        out_shape=(
            jax.ShapeDtypeStruct((2, 8 * W), F32),
            jax.ShapeDtypeStruct((8 * W, 256), BF),
            jax.ShapeDtypeStruct((1, 256), F32),
            jax.ShapeDtypeStruct((256, 8 * W), BF),
        ),
        in_specs=[vm] * 6,
        out_specs=[vm] * 4,
        scratch_shapes=[
            pltpu.VMEM((8, 4, W), F32),
            pltpu.VMEM((8, 4, W), F32),
            pltpu.VMEM((2, 16, W), F32),
            pltpu.VMEM((8, 2, W), F32),
            pltpu.VMEM((2, 64, 4, 16, W), BF),
            pltpu.VMEM((2, 64, 4, 16, W), BF),
            pltpu.VMEM((8, W, 1024), BF),
            pltpu.VMEM((8, 128, 256), BF),
            pltpu.VMEM((8, W, 256), BF),
            pltpu.VMEM((8, W, 256), BF),
            pltpu.VMEM((2, 512, 256), F32),
            pltpu.VMEM((2, 512, 256), F32),
            pltpu.VMEM((2, 512, 256), BF),
            pltpu.VMEM((2, 256, 512), BF),
            pltpu.VMEM((2, 512, 256), BF),
            pltpu.VMEM((2, 4, 8, 16, W), F32),
            pltpu.VMEM((4, 8, 16, W), F32),
            pltpu.VMEM((4, 8, 16, W), BF),
            pltpu.VMEM((4, 8, 16, W), BF),
            pltpu.VMEM((8, 16, W), BF),
            pltpu.VMEM((8, 16, W), BF),
            pltpu.VMEM((8, 2, W), F32),
            pltpu.SemaphoreType.DMA((144,)),
            pltpu.SemaphoreType.DMA((144,)),
        ],
        compiler_params=pltpu.CompilerParams(
            collective_id=0, has_side_effects=True, vmem_limit_bytes=56 * 1024 * 1024),
    )(source, target, enc_weight, enc_bias.reshape(1, 256), dec_weight.T, active)
    return (err, ge, gb.reshape(256), gd)


def solution(mesh):
    placed = (
        P(("tok", "feat"), None),
        P(("tok", "feat"), None),
        P("tok", "feat"),
        P("feat"),
        P("feat", "tok"),
        P("tok", "feat"),
    )
    return jax.shard_map(
        on_device,
        mesh=mesh,
        in_specs=placed,
        out_specs=(P(("tok", "feat"), None), P(None, "feat"), P("feat"), P("feat", None)),
        check_vma=False,
    )
```

```python
import math

import jax
import jax.numpy as jnp
from jax import lax
from jax.experimental import pallas as pl
from jax.experimental.pallas import tpu as pltpu
from jax.sharding import PartitionSpec as P

BF = jnp.bfloat16
F32 = jnp.float32
W = 448


def kernel(src_ref, tgt_ref, enc_ref, bias_ref, dec_ref, act_ref, err_ref, ge_ref, gb_ref, gd_ref,
           st_ref, st_in, st_rows, err_in, S, G, ST, at, wt, dt, gate, pre, feats, fT, prnd, part, r0, pb, r1, qb, r2, ebuf, ss, rs):
    tok = lax.axis_index("tok")
    feat = lax.axis_index("feat")
    zh, x = tok // 4, tok % 4
    zlo, y, c = feat // 8, (feat // 2) % 4, feat % 2
    z = zh * 8 + zlo
    zq, zr = z // 4, z % 4

    def dev(x_=None, y_=None, z_=None, c_=None):
        x_ = x if x_ is None else x_
        y_ = y if y_ is None else y_
        z_ = z if z_ is None else z_
        c_ = c if c_ is None else c_
        return {"tok": (z_ // 8) * 4 + x_, "feat": ((z_ % 8) * 4 + y_) * 2 + c_}

    def tok_dev(d):
        return {"tok": (tok + d) % 8, "feat": feat}

    zoff = (1, 15, 2)
    zback = (15, 1, 14)

    barrier = pltpu.get_barrier_semaphore()
    greet = [tok_dev(d) for d in range(1, 8)]
    greet += [dev(z_=(z + 4 * d) % 16) for d in (1, 3)]
    greet += [dev(z_=(z + d) % 16) for d in zback]
    greet += [dev(y_=(y + d) % 4) for d in (1, 2, 3)]
    greet += [dev(c_=1 - c)]
    greet += [dev(z_=zh * 8 + (zlo + d) % 8) for d in range(1, 8)]
    for g in greet:
        pl.semaphore_signal(barrier, inc=1, device_id=g, device_id_type=pl.DeviceIdType.MESH)

    nxt = [0]
    sent = []

    def send(src, dst, to):
        i = nxt[0]
        nxt[0] += 1
        cp = pltpu.make_async_remote_copy(
            src_ref=src, dst_ref=dst, send_sem=ss.at[i], recv_sem=rs.at[i],
            device_id=to, device_id_type=pl.DeviceIdType.MESH)
        cp.start()
        sent.append(cp)
        return cp

    def arrive(cps):
        for cp in cps:
            cp.wait_recv()

    me = x * 2 + zh
    across = dev(z_=(z + 8) % 16)
    wt[me] = enc_ref[...]
    at[me] = act_ref[...].astype(F32).astype(BF)
    dt[me] = dec_ref[...]
    rows_in = jnp.concatenate([src_ref[...].astype(F32), tgt_ref[...].astype(F32)], axis=0)
    for k in range(8):
        st_ref[k] = rows_in[:, k * W:k * W + W]
    pl.semaphore_wait(barrier, len(greet))

    def ring_start(piece, axis):
        p = {"x_": x, "y_": y}[axis]
        fwd, bwd = dev(**{axis: (p + 1) % 4}), dev(**{axis: (p + 3) % 4})
        own = [piece(p, 0), piece(p, 1)]
        a = send(own[0], own[0], fwd)
        b = send(own[1], own[1], bwd)
        late = [send(own[1], own[1], fwd), send(own[0], own[0], bwd)]
        return piece, p, fwd, bwd, a, b, late

    def ring_pass(state):
        piece, p, fwd, bwd, a, b, late = state
        arrive([a])
        left = piece((p + 3) % 4, 0)
        f = send(left, left, fwd)
        arrive([b])
        right = piece((p + 1) % 4, 1)
        g = send(right, right, bwd)
        return late, [f, g]

    def w_piece(buf, side):
        return lambda xx, half: buf.at[2 * xx + side, pl.ds(half * (W // 2), W // 2)]

    zl = zq % 2
    b0 = ((c * 4 + y) * 4 + x) * 2
    b1 = ((c * 4 + x) * 4 + y) * 2
    gi = b0 + zl * (b1 - b0) + zh

    def far(buf):
        own = buf.at[zl, gi, zr]
        return [send(own, own, dev(z_=(z + 4 * d) % 16)) for d in (2, 1, 3)]

    def near(buf):
        cols = [buf.at[0, pl.ds(b0, 2), zr], buf.at[1, pl.ds(b1, 2), zr]]
        return [send(q, q, dev(z_=(z + d) % 16)) for d in zoff for q in cols]

    def light(buf):
        q0, q1 = buf.at[0, pl.ds(b0, 2)], buf.at[1, pl.ds(b1, 2)]
        out = []
        for d in (1, 3, 2):
            out.append(send(q0, q0, dev(x_=(x + d) % 4)))
            out.append(send(q1, q1, dev(y_=(y + d) % 4)))
        return out

    def heavy(buf, half_no):
        return lambda p, half: buf.at[half_no, pl.ds((c * 4 + p) * 8 + half * 4, 4)]

    def swap(buf, half_no, p):
        q = buf.at[half_no, pl.ds((c * 4 + p) * 8, 8)]
        return send(q, q, dev(c_=1 - c))

    ex = [send(st_ref.at[(tok + d) % 8], st_in.at[tok], tok_dev(d)) for d in range(1, 8)]
    az = send(at.at[me], at.at[me], across)
    w0 = ring_start(w_piece(wt, zh), "x_")

    def w_part(i):
        q = wt.at[me, pl.ds(i * (W // 4), W // 4)]
        return send(q, q, across)

    st_in[tok] = st_ref[tok]
    arrive(ex)
    for k in range(8):
        v = st_in[k]
        st_rows[0, 2 * k:2 * k + 2, :] = v[0:2]
        st_rows[1, 2 * k:2 * k + 2, :] = v[2:4]
    S[zl, gi, zr] = st_rows[0].astype(BF)
    sz = far(S)
    wz = [w_part(0), w_part(1)]
    arrive(sz)
    sn = near(S)
    arrive([az])
    apair = at.at[pl.ds(2 * x, 2)]
    ax = [send(apair, apair, dev(x_=(x + d) % 4)) for d in (1, 3, 2)]
    w0l, w0f = ring_pass(w0)
    arrive(sn)
    one = light(S)
    wz += [w_part(2), w_part(3)]
    arrive(one)
    ra = ring_start(heavy(S, 0), "y_")
    rb = ring_start(heavy(S, 1), "x_")
    sc = [swap(S, 0, y), swap(S, 1, x)]
    arrive(ax)

    def order(h):
        n = lax.broadcasted_iota(jnp.int32, (512, 128), 0)
        m = lax.broadcasted_iota(jnp.int32, (512, 128), 1)
        fidx = ((((n >> 4) & 7) * 4 + (n >> 7)) * 2) + h
        slot = jnp.where(m == fidx * 2 + (n & 1), (n >> 1) & 7, 8)
        acc = jnp.zeros((512, 256), F32)
        for t in range(8):
            perm = jnp.where(slot == t, 1.0, 0.0).astype(BF)
            acc += jnp.dot(perm, at[(t % 4) * 2 + t // 4], preferred_element_type=F32)
        gate[h] = acc

    order(0)
    al, af = ring_pass(ra)
    bl, bf = ring_pass(rb)
    order(1)
    arrive(w0l)
    arrive(w0f)
    dz = send(dt.at[me], dt.at[me], across)
    arrive(wz)
    w1 = ring_start(w_piece(wt, 1 - zh), "x_")

    def rows(buf, h, k):
        parts = []
        for yy in range(4):
            parts.append(buf[0, ((h * 4 + yy) * 4 + k // 2) * 2 + k % 2].reshape(64, W))
            parts.append(buf[1, ((h * 4 + k // 2) * 4 + yy) * 2 + k % 2].reshape(64, W))
        return jnp.concatenate(parts, axis=0)

    def encode(h, side):
        def step(i, _):
            pre[h] += jnp.dot(rows(S, h, 2 * i + side), wt[2 * i + side], preferred_element_type=F32)
            return 0

        lax.fori_loop(0, 4, step, 0, unroll=2)

    def finish(h):
        feats[h] = (gate[h] * (pre[h] + bias_ref[...])).astype(BF)

    def decode(h):
        r = lax.dot_general(feats[h], dt[me], (((1,), (1,)), ((), ())), preferred_element_type=F32)
        part[h] = r.reshape(4, 8, 16, W)

    arrive(al)
    arrive(bl)
    sc += [swap(S, 0, (y + 1) % 4), swap(S, 0, (y + 3) % 4), swap(S, 1, (x + 1) % 4), swap(S, 1, (x + 3) % 4)]
    arrive(af)
    sc.append(swap(S, 0, (y + 2) % 4))
    arrive(bf)
    sc.append(swap(S, 1, (x + 2) % 4))
    w1l, w1f = ring_pass(w1)
    d0 = ring_start(w_piece(dt, zh), "x_")
    pre[...] = jnp.zeros((2, 512, 256), F32)
    encode(c, zh)
    arrive(sc)
    encode(1 - c, zh)
    arrive(w1l)
    arrive(w1f)
    encode(1 - c, 1 - zh)
    finish(1 - c)
    decode(1 - c)
    pc = [send(part.at[1 - c, (y + d) % 4], r0.at[(y + d) % 4], dev(c_=1 - c)) for d in (2, 1, 3, 0)]
    encode(c, 1 - zh)
    finish(c)
    d0l, d0f = ring_pass(d0)
    decode(c)
    py = []
    for i, d in enumerate((2, 1, 3)):
        yy = (y + d) % 4
        arrive([pc[i]])
        pb[yy] = (part[c, yy] + r0[yy]).astype(BF)
        py.append(send(pb.at[yy], r1.at[d], dev(y_=yy)))
    arrive([pc[3]])
    def turn(k, _):
        ST[k] = jnp.concatenate([rows(S, 0, k), rows(S, 1, k)], axis=0).T
        return 0

    for h in range(2):
        fT[:, h * 512:h * 512 + 512] = feats[h].T
    lax.fori_loop(0, 1, turn, 0)
    arrive(py)
    total = part[c, y] + r0[y] + r1[1].astype(F32) + r1[2].astype(F32) + r1[3].astype(F32)
    part[c, y] = total
    qb[...] = total.astype(BF)
    pz = [send(qb.at[(zlo + d) % 8], r2.at[d], dev(z_=zh * 8 + (zlo + d) % 8)) for d in (4, 3, 5, 2, 6, 1, 7)]
    arrive([dz])
    d1 = ring_start(w_piece(dt, 1 - zh), "x_")
    lax.fori_loop(1, 4, turn, 0)
    arrive(pz)
    recon = part[c, y, zlo]
    for d in range(1, 8):
        recon = recon + r2[d].astype(F32)
    err = recon - st_rows[1]

    G[zl, gi, zr] = (err * (1.0 / 32.0)).astype(BF)
    gz = far(G)
    for k in range(8):
        ebuf[k] = err[2 * k:2 * k + 2]
    err_in[tok] = ebuf[tok]
    eo = [send(ebuf.at[(tok + d) % 8], err_in.at[tok], tok_dev(d)) for d in range(1, 8)]
    d1l, d1f = ring_pass(d1)
    lax.fori_loop(4, 6, turn, 0)
    arrive(gz)
    arrive(near(G))
    arrive(light(G))
    ra = ring_start(heavy(G, 0), "y_")
    rb = ring_start(heavy(G, 1), "x_")
    gc = [swap(G, 0, y), swap(G, 1, x)]

    lax.fori_loop(6, 8, turn, 0)
    al, af = ring_pass(ra)
    bl, bf = ring_pass(rb)
    for cps in (d0l, d0f, d1l, d1f):
        arrive(cps)
    arrive(al)
    arrive(bl)
    gc += [swap(G, 0, (y + 1) % 4), swap(G, 0, (y + 3) % 4), swap(G, 1, (x + 1) % 4), swap(G, 1, (x + 3) % 4)]
    arrive(af)
    gc.append(swap(G, 0, (y + 2) % 4))
    arrive(bf)
    gc.append(swap(G, 1, (x + 2) % 4))

    def back(h):
        pre[h] = jnp.zeros((512, 256), F32)

        def step(k, _):
            pre[h] += jnp.dot(rows(G, h, k), dt[k], preferred_element_type=F32)
            return 0

        lax.fori_loop(0, 8, step, 0, unroll=2)
        g = gate[h] * pre[h]
        prnd[h] = g.astype(BF)
        return jnp.sum(g, axis=0, keepdims=True)

    bsum = back(c)
    arrive(gc)
    gb_ref[...] = bsum + back(1 - c)

    def grads(n, _):
        halves = []
        for odd in range(2):
            t = 2 * n + odd
            k = (t % 4) * 2 + t // 4
            ge = jnp.dot(ST[k], prnd[...].reshape(1024, 256), preferred_element_type=F32)
            gd = jnp.dot(fT[...], jnp.concatenate([rows(G, 0, k), rows(G, 1, k)], axis=0),
                         preferred_element_type=F32)
            ge_ref[pl.ds(pl.multiple_of(t * W, W), W), :] = ge.astype(BF)
            halves.append(gd)
        both = jnp.concatenate(halves, axis=1).astype(BF)
        gd_ref[:, pl.ds(pl.multiple_of(n * 2 * W, 2 * W), 2 * W)] = both
        return 0

    arrive(eo)
    err_ref[...] = jnp.concatenate([err_in[k] for k in range(8)], axis=1)
    lax.fori_loop(0, 4, grads, 0)
    for cp in sent:
        cp.wait_send()


def on_device(source, target, enc_weight, enc_bias, dec_weight, active):
    vm = pl.BlockSpec(memory_space=pltpu.VMEM)
    err, ge, gb, gd = pl.pallas_call(
        kernel,
        out_shape=(
            jax.ShapeDtypeStruct((2, 8 * W), F32),
            jax.ShapeDtypeStruct((8 * W, 256), BF),
            jax.ShapeDtypeStruct((1, 256), F32),
            jax.ShapeDtypeStruct((256, 8 * W), BF),
        ),
        in_specs=[vm] * 6,
        out_specs=[vm] * 4,
        scratch_shapes=[
            pltpu.VMEM((8, 4, W), F32),
            pltpu.VMEM((8, 4, W), F32),
            pltpu.VMEM((2, 16, W), F32),
            pltpu.VMEM((8, 2, W), F32),
            pltpu.VMEM((2, 64, 4, 16, W), BF),
            pltpu.VMEM((2, 64, 4, 16, W), BF),
            pltpu.VMEM((8, W, 1024), BF),
            pltpu.VMEM((8, 128, 256), BF),
            pltpu.VMEM((8, W, 256), BF),
            pltpu.VMEM((8, W, 256), BF),
            pltpu.VMEM((2, 512, 256), F32),
            pltpu.VMEM((2, 512, 256), F32),
            pltpu.VMEM((2, 512, 256), BF),
            pltpu.VMEM((256, 1024), BF),
            pltpu.VMEM((2, 512, 256), BF),
            pltpu.VMEM((2, 4, 8, 16, W), F32),
            pltpu.VMEM((4, 8, 16, W), F32),
            pltpu.VMEM((4, 8, 16, W), BF),
            pltpu.VMEM((4, 8, 16, W), BF),
            pltpu.VMEM((8, 16, W), BF),
            pltpu.VMEM((8, 16, W), BF),
            pltpu.VMEM((8, 2, W), F32),
            pltpu.SemaphoreType.DMA((144,)),
            pltpu.SemaphoreType.DMA((144,)),
        ],
        compiler_params=pltpu.CompilerParams(
            collective_id=0, has_side_effects=True, vmem_limit_bytes=56 * 1024 * 1024),
    )(source, target, enc_weight, enc_bias.reshape(1, 256), dec_weight.T, active)
    return (err, ge, gb.reshape(256), gd)


def solution(mesh):
    placed = (
        P(("tok", "feat"), None),
        P(("tok", "feat"), None),
        P("tok", "feat"),
        P("feat"),
        P("feat", "tok"),
        P("tok", "feat"),
    )
    return jax.shard_map(
        on_device,
        mesh=mesh,
        in_specs=placed,
        out_specs=(P(("tok", "feat"), None), P(None, "feat"), P("feat"), P("feat", None)),
        check_vma=False,
    )
```

```python
import math

import jax
import jax.numpy as jnp
from jax import lax
from jax.experimental import pallas as pl
from jax.experimental.pallas import tpu as pltpu
from jax.sharding import PartitionSpec as P

BF = jnp.bfloat16
F32 = jnp.float32
W = 448


def kernel(src_ref, tgt_ref, enc_ref, bias_ref, dec_ref, act_ref, err_ref, ge_ref, gb_ref, gd_ref,
           st_ref, st_in, st_rows, err_in, S, G, ST, at, wt, dt, gate, pre, feats, fT, prnd, part, r0, pb, r1, qb, r2, ebuf, ss, rs):
    tok = lax.axis_index("tok")
    feat = lax.axis_index("feat")
    zh, x = tok // 4, tok % 4
    zlo, y, c = feat // 8, (feat // 2) % 4, feat % 2
    z = zh * 8 + zlo
    zq, zr = z // 4, z % 4

    def dev(x_=None, y_=None, z_=None, c_=None):
        x_ = x if x_ is None else x_
        y_ = y if y_ is None else y_
        z_ = z if z_ is None else z_
        c_ = c if c_ is None else c_
        return {"tok": (z_ // 8) * 4 + x_, "feat": ((z_ % 8) * 4 + y_) * 2 + c_}

    def tok_dev(d):
        return {"tok": (tok + d) % 8, "feat": feat}

    zoff = (1, 15, 2)
    zback = (15, 1, 14)

    barrier = pltpu.get_barrier_semaphore()
    greet = [tok_dev(d) for d in range(1, 8)]
    greet += [dev(z_=(z + 4 * d) % 16) for d in (1, 3)]
    greet += [dev(z_=(z + d) % 16) for d in zback]
    greet += [dev(y_=(y + d) % 4) for d in (1, 2, 3)]
    greet += [dev(c_=1 - c)]
    greet += [dev(z_=zh * 8 + (zlo + d) % 8) for d in range(1, 8)]
    for g in greet:
        pl.semaphore_signal(barrier, inc=1, device_id=g, device_id_type=pl.DeviceIdType.MESH)

    nxt = [0]
    sent = []

    def send(src, dst, to):
        i = nxt[0]
        nxt[0] += 1
        cp = pltpu.make_async_remote_copy(
            src_ref=src, dst_ref=dst, send_sem=ss.at[i], recv_sem=rs.at[i],
            device_id=to, device_id_type=pl.DeviceIdType.MESH)
        cp.start()
        sent.append(cp)
        return cp

    def arrive(cps):
        for cp in cps:
            cp.wait_recv()

    me = x * 2 + zh
    across = dev(z_=(z + 8) % 16)
    wt[me] = enc_ref[...]
    at[me] = act_ref[...].astype(F32).astype(BF)
    dt[me] = dec_ref[...]
    rows_in = jnp.concatenate([src_ref[...].astype(F32), tgt_ref[...].astype(F32)], axis=0)
    for k in range(8):
        st_ref[k] = rows_in[:, k * W:k * W + W]
    pl.semaphore_wait(barrier, len(greet))

    def ring_start(piece, axis):
        p = {"x_": x, "y_": y}[axis]
        fwd, bwd = dev(**{axis: (p + 1) % 4}), dev(**{axis: (p + 3) % 4})
        own = [piece(p, 0), piece(p, 1)]
        a = send(own[0], own[0], fwd)
        b = send(own[1], own[1], bwd)
        late = [send(own[1], own[1], fwd), send(own[0], own[0], bwd)]
        return piece, p, fwd, bwd, a, b, late

    def ring_pass(state):
        piece, p, fwd, bwd, a, b, late = state
        arrive([a])
        left = piece((p + 3) % 4, 0)
        f = send(left, left, fwd)
        arrive([b])
        right = piece((p + 1) % 4, 1)
        g = send(right, right, bwd)
        return late, [f, g]

    def w_piece(buf, side):
        return lambda xx, half: buf.at[2 * xx + side, pl.ds(half * (W // 2), W // 2)]

    zl = zq % 2
    b0 = ((c * 4 + y) * 4 + x) * 2
    b1 = ((c * 4 + x) * 4 + y) * 2
    gi = b0 + zl * (b1 - b0) + zh

    def far(buf):
        own = buf.at[zl, gi, zr]
        return [send(own, own, dev(z_=(z + 4 * d) % 16)) for d in (2, 1, 3)]

    def near(buf):
        cols = [buf.at[0, pl.ds(b0, 2), zr], buf.at[1, pl.ds(b1, 2), zr]]
        return [send(q, q, dev(z_=(z + d) % 16)) for d in zoff for q in cols]

    def light(buf):
        q0, q1 = buf.at[0, pl.ds(b0, 2)], buf.at[1, pl.ds(b1, 2)]
        out = []
        for d in (1, 3, 2):
            out.append(send(q0, q0, dev(x_=(x + d) % 4)))
            out.append(send(q1, q1, dev(y_=(y + d) % 4)))
        return out

    def heavy(buf, half_no):
        return lambda p, half: buf.at[half_no, pl.ds((c * 4 + p) * 8 + half * 4, 4)]

    def swap(buf, half_no, p):
        q = buf.at[half_no, pl.ds((c * 4 + p) * 8, 8)]
        return send(q, q, dev(c_=1 - c))

    ex = [send(st_ref.at[(tok + d) % 8], st_in.at[tok], tok_dev(d)) for d in range(1, 8)]
    az = send(at.at[me], at.at[me], across)
    w0 = ring_start(w_piece(wt, zh), "x_")

    def w_part(i):
        q = wt.at[me, pl.ds(i * (W // 4), W // 4)]
        return send(q, q, across)

    st_in[tok] = st_ref[tok]
    arrive(ex)
    for k in range(8):
        v = st_in[k]
        st_rows[0, 2 * k:2 * k + 2, :] = v[0:2]
        st_rows[1, 2 * k:2 * k + 2, :] = v[2:4]
    S[zl, gi, zr] = st_rows[0].astype(BF)
    sz = far(S)
    wz = [w_part(0), w_part(1)]
    arrive(sz)
    sn = near(S)
    arrive([az])
    apair = at.at[pl.ds(2 * x, 2)]
    ax = [send(apair, apair, dev(x_=(x + d) % 4)) for d in (1, 3, 2)]
    w0l, w0f = ring_pass(w0)
    arrive(sn)
    one = light(S)
    wz += [w_part(2), w_part(3)]
    arrive(one)
    ra = ring_start(heavy(S, 0), "y_")
    rb = ring_start(heavy(S, 1), "x_")
    sc = [swap(S, 0, y), swap(S, 1, x)]
    arrive(ax)

    def order(h):
        n = lax.broadcasted_iota(jnp.int32, (512, 128), 0)
        m = lax.broadcasted_iota(jnp.int32, (512, 128), 1)
        fidx = ((((n >> 4) & 7) * 4 + (n >> 7)) * 2) + h
        slot = jnp.where(m == fidx * 2 + (n & 1), (n >> 1) & 7, 8)
        acc = jnp.zeros((512, 256), F32)
        for t in range(8):
            perm = jnp.where(slot == t, 1.0, 0.0).astype(BF)
            acc += jnp.dot(perm, at[(t % 4) * 2 + t // 4], preferred_element_type=F32)
        gate[h] = acc

    order(0)
    al, af = ring_pass(ra)
    bl, bf = ring_pass(rb)
    arrive(w0l)
    arrive(w0f)
    dz = send(dt.at[me], dt.at[me], across)
    arrive(wz)
    w1 = ring_start(w_piece(wt, 1 - zh), "x_")
    order(1)

    def rows(buf, h, k):
        parts = []
        for yy in range(4):
            parts.append(buf[0, ((h * 4 + yy) * 4 + k // 2) * 2 + k % 2].reshape(64, W))
            parts.append(buf[1, ((h * 4 + k // 2) * 4 + yy) * 2 + k % 2].reshape(64, W))
        return jnp.concatenate(parts, axis=0)

    def encode(h, side):
        def step(i, _):
            pre[h] += jnp.dot(rows(S, h, 2 * i + side), wt[2 * i + side], preferred_element_type=F32)
            return 0

        lax.fori_loop(0, 4, step, 0, unroll=2)

    def finish(h):
        feats[h] = (gate[h] * (pre[h] + bias_ref[...])).astype(BF)

    def decode(h):
        r = lax.dot_general(feats[h], dt[me], (((1,), (1,)), ((), ())), preferred_element_type=F32)
        part[h] = r.reshape(4, 8, 16, W)

    arrive(al)
    arrive(bl)
    sc += [swap(S, 0, (y + 1) % 4), swap(S, 0, (y + 3) % 4), swap(S, 1, (x + 1) % 4), swap(S, 1, (x + 3) % 4)]
    arrive(af)
    sc.append(swap(S, 0, (y + 2) % 4))
    arrive(bf)
    sc.append(swap(S, 1, (x + 2) % 4))
    w1l, w1f = ring_pass(w1)
    d0 = ring_start(w_piece(dt, zh), "x_")
    pre[...] = jnp.zeros((2, 512, 256), F32)
    encode(c, zh)
    arrive(sc)
    encode(1 - c, zh)
    arrive(w1l)
    arrive(w1f)
    encode(1 - c, 1 - zh)
    finish(1 - c)
    decode(1 - c)
    pc = [send(part.at[1 - c, (y + d) % 4], r0.at[(y + d) % 4], dev(c_=1 - c)) for d in (2, 1, 3, 0)]
    encode(c, 1 - zh)
    finish(c)
    d0l, d0f = ring_pass(d0)
    decode(c)
    py = []
    for i, d in enumerate((2, 1, 3)):
        yy = (y + d) % 4
        arrive([pc[i]])
        pb[yy] = (part[c, yy] + r0[yy]).astype(BF)
        py.append(send(pb.at[yy], r1.at[d], dev(y_=yy)))
    arrive([pc[3]])
    def turn(k, _):
        ST[k] = jnp.concatenate([rows(S, 0, k), rows(S, 1, k)], axis=0).T
        return 0

    for h in range(2):
        fT[:, h * 512:h * 512 + 512] = feats[h].T
    lax.fori_loop(0, 1, turn, 0)
    arrive(py)
    total = part[c, y] + r0[y] + r1[1].astype(F32) + r1[2].astype(F32) + r1[3].astype(F32)
    part[c, y] = total
    qb[...] = total.astype(BF)
    pz = [send(qb.at[(zlo + d) % 8], r2.at[d], dev(z_=zh * 8 + (zlo + d) % 8)) for d in (4, 3, 5, 2, 6, 1, 7)]
    arrive([dz])
    d1 = ring_start(w_piece(dt, 1 - zh), "x_")
    lax.fori_loop(1, 4, turn, 0)
    arrive(pz)
    recon = part[c, y, zlo]
    for d in range(1, 8):
        recon = recon + r2[d].astype(F32)
    err = recon - st_rows[1]

    G[zl, gi, zr] = (err * (1.0 / 32.0)).astype(BF)
    gz = far(G)
    for k in range(8):
        ebuf[k] = err[2 * k:2 * k + 2]
    err_in[tok] = ebuf[tok]
    eo = [send(ebuf.at[(tok + d) % 8], err_in.at[tok], tok_dev(d)) for d in range(1, 8)]
    d1l, d1f = ring_pass(d1)
    lax.fori_loop(4, 6, turn, 0)
    arrive(gz)
    arrive(near(G))
    arrive(light(G))
    ra = ring_start(heavy(G, 0), "y_")
    rb = ring_start(heavy(G, 1), "x_")
    gc = [swap(G, 0, y), swap(G, 1, x)]

    lax.fori_loop(6, 8, turn, 0)
    al, af = ring_pass(ra)
    bl, bf = ring_pass(rb)
    for cps in (d0l, d0f, d1l, d1f):
        arrive(cps)
    arrive(al)
    arrive(bl)
    gc += [swap(G, 0, (y + 1) % 4), swap(G, 0, (y + 3) % 4), swap(G, 1, (x + 1) % 4), swap(G, 1, (x + 3) % 4)]
    arrive(af)
    gc.append(swap(G, 0, (y + 2) % 4))
    arrive(bf)
    gc.append(swap(G, 1, (x + 2) % 4))

    def back(h):
        pre[h] = jnp.zeros((512, 256), F32)

        def step(k, _):
            pre[h] += jnp.dot(rows(G, h, k), dt[k], preferred_element_type=F32)
            return 0

        lax.fori_loop(0, 8, step, 0, unroll=2)
        g = gate[h] * pre[h]
        prnd[h] = g.astype(BF)
        return jnp.sum(g, axis=0, keepdims=True)

    bsum = back(c)
    arrive(gc)
    gb_ref[...] = bsum + back(1 - c)

    def grads(n, _):
        halves = []
        for odd in range(2):
            t = 2 * n + odd
            k = (t % 4) * 2 + t // 4
            ge = jnp.dot(ST[k], prnd[...].reshape(1024, 256), preferred_element_type=F32)
            gd = jnp.dot(fT[...], jnp.concatenate([rows(G, 0, k), rows(G, 1, k)], axis=0),
                         preferred_element_type=F32)
            ge_ref[pl.ds(pl.multiple_of(t * W, W), W), :] = ge.astype(BF)
            halves.append(gd)
        both = jnp.concatenate(halves, axis=1).astype(BF)
        gd_ref[:, pl.ds(pl.multiple_of(n * 2 * W, 2 * W), 2 * W)] = both
        return 0

    arrive(eo)
    err_ref[...] = jnp.concatenate([err_in[k] for k in range(8)], axis=1)
    lax.fori_loop(0, 4, grads, 0)
    for cp in sent:
        cp.wait_send()


def on_device(source, target, enc_weight, enc_bias, dec_weight, active):
    vm = pl.BlockSpec(memory_space=pltpu.VMEM)
    err, ge, gb, gd = pl.pallas_call(
        kernel,
        out_shape=(
            jax.ShapeDtypeStruct((2, 8 * W), F32),
            jax.ShapeDtypeStruct((8 * W, 256), BF),
            jax.ShapeDtypeStruct((1, 256), F32),
            jax.ShapeDtypeStruct((256, 8 * W), BF),
        ),
        in_specs=[vm] * 6,
        out_specs=[vm] * 4,
        scratch_shapes=[
            pltpu.VMEM((8, 4, W), F32),
            pltpu.VMEM((8, 4, W), F32),
            pltpu.VMEM((2, 16, W), F32),
            pltpu.VMEM((8, 2, W), F32),
            pltpu.VMEM((2, 64, 4, 16, W), BF),
            pltpu.VMEM((2, 64, 4, 16, W), BF),
            pltpu.VMEM((8, W, 1024), BF),
            pltpu.VMEM((8, 128, 256), BF),
            pltpu.VMEM((8, W, 256), BF),
            pltpu.VMEM((8, W, 256), BF),
            pltpu.VMEM((2, 512, 256), F32),
            pltpu.VMEM((2, 512, 256), F32),
            pltpu.VMEM((2, 512, 256), BF),
            pltpu.VMEM((256, 1024), BF),
            pltpu.VMEM((2, 512, 256), BF),
            pltpu.VMEM((2, 4, 8, 16, W), F32),
            pltpu.VMEM((4, 8, 16, W), F32),
            pltpu.VMEM((4, 8, 16, W), BF),
            pltpu.VMEM((4, 8, 16, W), BF),
            pltpu.VMEM((8, 16, W), BF),
            pltpu.VMEM((8, 16, W), BF),
            pltpu.VMEM((8, 2, W), F32),
            pltpu.SemaphoreType.DMA((144,)),
            pltpu.SemaphoreType.DMA((144,)),
        ],
        compiler_params=pltpu.CompilerParams(
            collective_id=0, has_side_effects=True, vmem_limit_bytes=56 * 1024 * 1024),
    )(source, target, enc_weight, enc_bias.reshape(1, 256), dec_weight.T, active)
    return (err, ge, gb.reshape(256), gd)


def solution(mesh):
    placed = (
        P(("tok", "feat"), None),
        P(("tok", "feat"), None),
        P("tok", "feat"),
        P("feat"),
        P("feat", "tok"),
        P("tok", "feat"),
    )
    return jax.shard_map(
        on_device,
        mesh=mesh,
        in_specs=placed,
        out_specs=(P(("tok", "feat"), None), P(None, "feat"), P("feat"), P("feat", None)),
        check_vma=False,
    )
```
